512 devices in a mesh: ref: 32 (over z, core), qry: 16 (over x, y).
Axes of the slice: x: 4, y: 4, z: 16, core: 2. Of those that a mesh axis runs over, the one named last changes fastest.
Arguments:
- queries: bfloat16 [4096, 1024], P('qry'), may hold values from -1 to 1
- ref_panels: bfloat16 [256, 128, 1024], P('ref', 'qry'), may hold values from -1 to 1
- cand_mask: int32 [32, 256], P('qry', 'ref'), may hold values 0 or 1
- panel_time: int32 [256], replicated, may hold values from 0 to 255, as said below
- w_first: float32 [9, 32], replicated, may hold values from -2 to 2
- b_first: float32 [32], replicated, may hold values from -2.5 to 2.5
- w_second: bfloat16 [9, 32], replicated, may hold values from -0.375 to 0.375
Outputs:
- score_map: bfloat16 [4096, 32768], P('qry', 'ref')
The draws below stay inside these ranges and needn't reach their ends.
Inputs may be any that keep to these rules, and one draw needn't show every extreme that they name: `panel_time`: A permutation of the reference time blocks. The owner of block t is t // 8; every owner has 8 blocks. The 8 panels of one ingest index of ref (panels held by one index) include at most 1 of one owner, and every ingest index has 1 panel of some owner.
All inputs are finite; a program needn't handle non-finite values. No bound on the sum of `cand_mask` on one device may be relied on, other than what follows from the above.
Results may differ from the reference program's by a relative error of at most 0.0059.
Values may be sent and summed in bfloat16 or wider, within the bound.
No kernel may reach another device: no remote copies, remote signals or barrier semaphores. Data moves between devices by JAX's collectives and lax.ppermute only.
A program may use at most 64 MiB of HBM per device.

```python
import math
import jax
import jax.numpy as jnp
from jax import lax

D = 1024
C1 = 32
PR = 128
QB = 128
FRAMES = 256
RB_DEV = 8
SLOT = 1
NPANELS = 256
QFRAMES = 4096
QBLOCKS = 32


def draw_panel_time(key, part):
    keys = jax.random.split(key, 5)
    owners_count = NPANELS // RB_DEV
    values = jax.random.permutation(keys[0], owners_count)
    position = jnp.arange(RB_DEV)
    choose = position // SLOT
    offsets = values[choose]
    shifter = jax.random.permutation(keys[1], owners_count)
    relabel = jax.random.permutation(keys[2], owners_count)
    orders = jax.vmap(lambda sub_key: jax.random.permutation(sub_key, RB_DEV))(jax.random.split(keys[3], owners_count))
    owner_ids = relabel[(shifter[:, None] + offsets[orders]) % owners_count]
    flat = owner_ids.reshape(-1)
    ranking = jax.random.permutation(keys[4], NPANELS)
    same_owner = flat[:, None] == flat[None, :]
    below = ranking[None, :] < ranking[:, None]
    within = jnp.sum(same_owner & below, axis=1)
    return (flat * RB_DEV + within).astype(jnp.int32)


def place_ends(values, own_key, least, high):
    place = [jax.random.randint(jax.random.fold_in(own_key, axis), (), 0, length) for axis, length in enumerate(values.shape)]
    widest = values.shape.index(max(values.shape))
    next_to = place[:widest] + [(place[widest] + 1) % values.shape[widest]] + place[widest + 1:]
    return values.at[tuple(place)].set(least).at[tuple(next_to)].set(high)


def shard_levels(key, dims, shards, smallest, high):
    level, own = 1.0, jax.random.fold_in(key, 6)
    for dim, shards_of in shards:
        heights = jnp.exp(jax.random.uniform(jax.random.fold_in(own, dim), (shards_of,), jnp.float32, smallest / len(shards), high / len(shards)))
        level = level * jnp.repeat(heights, dims[dim] // shards_of).reshape([-1 if axis == dim else 1 for axis in range(len(dims))])
    return level


def noise(key, extent, scale, reach, cuts=(), kind=jnp.bfloat16):
    entries = scale * jax.random.normal(key, extent, jnp.float32)
    if cuts:
        entries = entries * shard_levels(key, extent, cuts, -0.22, 0.18)
    return jnp.clip(entries, -reach, reach).astype(kind)


def setup_inputs(seed: int = 0) -> dict:
    streams_of = jax.random.split(jax.random.key(seed), 8)
    queries = noise(streams_of[0], (QFRAMES, D), 0.177, 1.0, ((0, 16),))
    ref_panels = noise(streams_of[1], (NPANELS, PR, D), 0.177, 1.0, ((0, 32), (1, 16)))
    cand_mask = place_ends((jax.random.randint(streams_of[2], (QBLOCKS, NPANELS), 0, 8) < 7).astype(jnp.int32), jax.random.fold_in(streams_of[2], 1), 0, 1)
    panel_time = draw_panel_time(jax.random.fold_in(streams_of[7], 71), 0)
    w_first = noise(streams_of[4], (9, C1), 9 ** -0.5, 2.0, (), jnp.float32)
    b_first = noise(streams_of[5], (C1,), 0.5, 2.5, (), jnp.float32)
    w_second = noise(streams_of[6], (9, C1), (9 * C1) ** -0.5, 0.375)
    return dict(queries=queries, ref_panels=ref_panels, cand_mask=cand_mask, panel_time=panel_time, w_first=w_first, b_first=b_first, w_second=w_second)


def layer_one(strip_cols, w_first, b_first):
    height = strip_cols.shape[0]
    widths = strip_cols.shape[1] - 2
    padded = jnp.pad(strip_cols.astype(jnp.float32), ((1, 1), (0, 0)))
    summed = jnp.broadcast_to(b_first[:, None, None], (b_first.shape[0], height, widths)).astype(jnp.float32)
    for row_shift in range(3):
        for col_shift in range(3):
            summed = summed + w_first[3 * row_shift + col_shift][:, None, None] * padded[row_shift:row_shift + height, col_shift:col_shift + widths][None]
    return jnp.maximum(summed, 0.0).astype(jnp.bfloat16)


def layer_two(hidden, w_second):
    height = hidden.shape[1]
    widths = hidden.shape[2] - 2
    padded = jnp.pad(hidden, ((0, 0), (1, 1), (0, 0))).astype(jnp.float32)
    weights = w_second.astype(jnp.float32)
    summed = jnp.zeros((height, widths), jnp.float32)
    for row_shift in range(3):
        for col_shift in range(3):
            summed = summed + jnp.einsum('c,chw->hw', weights[3 * row_shift + col_shift], padded[:, row_shift:row_shift + height, col_shift:col_shift + widths])
    return summed


def reference(queries, ref_panels, cand_mask, panel_time, w_first, b_first, w_second):
    npanel = ref_panels.shape[0]
    inverse = jnp.zeros((npanel,), jnp.int32).at[panel_time].set(jnp.arange(npanel, dtype=jnp.int32))
    slab = ref_panels[inverse].reshape(npanel * PR, D)
    total_cols = npanel * PR
    block_cols = math.gcd(1024, total_cols)
    count = total_cols // block_cols
    per_video_blocks = FRAMES // QB
    video_total = queries.shape[0] // FRAMES

    def per_video(video_index):
        video = lax.dynamic_slice_in_dim(queries, video_index * FRAMES, FRAMES, 0)
        masks = lax.dynamic_slice_in_dim(cand_mask, video_index * per_video_blocks, per_video_blocks, 0)
        sims = jnp.dot(video, slab.T, preferred_element_type=jnp.float32).astype(jnp.bfloat16)
        keeper = masks.astype(jnp.bfloat16)[:, None, :, None]
        sims = (sims.reshape(per_video_blocks, QB, npanel, PR) * keeper).reshape(FRAMES, total_cols)
        spread = jnp.pad(sims, ((0, 0), (2, 2)))

        def one_block(block_index):
            strip_cols = lax.dynamic_slice_in_dim(spread, block_index * block_cols, block_cols + 4, 1)
            hidden = layer_one(strip_cols, w_first, b_first)
            first = jnp.where(block_index == 0, jnp.zeros_like(hidden[:, :, 0]), hidden[:, :, 0])
            final = jnp.where(block_index == count - 1, jnp.zeros_like(hidden[:, :, -1]), hidden[:, :, -1])
            hidden = hidden.at[:, :, 0].set(first).at[:, :, -1].set(final)
            return layer_two(hidden, w_second).astype(jnp.bfloat16)

        blocks_out = lax.map(one_block, jnp.arange(count, dtype=jnp.int32))
        return jnp.transpose(blocks_out, (1, 0, 2)).reshape(FRAMES, total_cols)

    result = lax.map(per_video, jnp.arange(video_total, dtype=jnp.int32))
    return result.reshape(video_total * FRAMES, total_cols)
```

```python
import functools

import jax
import jax.numpy as jnp
import numpy as np
from jax import lax
from jax.experimental import pallas as pl
from jax.experimental.pallas import tpu as pltpu
from jax.sharding import PartitionSpec as P

BF = jnp.bfloat16
F = jnp.float32
I = jnp.int32
NT = (((1,), (1,)), ((), ()))
ROWS = 256
COLS = 1024
BLOCKS = 8
LANES = 128
WIN = 32
BPI = 4


def from_above(v):
    row = lax.broadcasted_iota(I, v.shape, 0)
    return jnp.where(row == 0, 0.0, pltpu.roll(v, 1, 0))


def from_below(v):
    row = lax.broadcasted_iota(I, v.shape, 0)
    n = v.shape[0]
    return jnp.where(row == n - 1, 0.0, pltpu.roll(v, n - 1, 0))


def quarters(lane, four):
    return jnp.where(
        lane < 64,
        jnp.where(lane < 32, four[0], four[1]),
        jnp.where(lane < 96, four[2], four[3]),
    )


def refine_body(
    mask_ref, slab_ref, q_hbm, sel1_hbm, w1_hbm, w2_hbm, sel2_hbm,
    out_ref, own_ref, part_ref, sims, gg, xs, hs, acc, ee, q_ref, sel1_ref, w1_ref, w2_ref, sel2_ref, sems,
):
    loads = [
        pltpu.make_async_copy(src, dst, sems.at[n])
        for n, (src, dst) in enumerate(
            zip((q_hbm, sel1_hbm, w1_hbm, w2_hbm, sel2_hbm), (q_ref, sel1_ref, w1_ref, w2_ref, sel2_ref))
        )
    ]
    for load in loads:
        load.start()
    loads[0].wait()
    loads[1].wait()
    lane = lax.broadcasted_iota(I, (ROWS, LANES), 1)
    top = lax.broadcasted_iota(I, (ROWS, LANES), 0) < ROWS // 2
    q = q_ref[...]
    g0 = jnp.zeros((ROWS, 2 * LANES), F)
    for t in range(0, BLOCKS, 2):
        slab = slab_ref[:, t : t + 2].swapaxes(0, 1).reshape(2 * LANES, q.shape[1])
        s = lax.dot_general(q, slab, NT, preferred_element_type=F)
        for u in range(2):
            keep = jnp.where(top, mask_ref[0, t + u], mask_ref[1, t + u]).astype(F)
            v = s[:, LANES * u : LANES * (u + 1)].astype(BF).astype(F) * keep
            sims[t + u] = v
            g0 = g0 + jnp.dot(
                v.astype(BF), sel1_ref[LANES * (t + u) : LANES * (t + u + 1), :], preferred_element_type=F
            )
    own_ref[...] = g0[:, :LANES]
    g = g0 + pltpu.roll(from_above(g0), 2 * LANES - 1, 1) + pltpu.roll(from_below(g0), 1, 1)
    gg[0] = g[:, :LANES]
    gg[1] = g[:, LANES:]
    ee[...] = jnp.zeros((2, ROWS, LANES), F)
    group = ROWS * BPI
    for load in loads[2:]:
        load.wait()

    def step(it, carry):
        for b in range(BPI):
            k = it * BPI + b
            s = sims[k]
            up = from_above(s)
            dn = from_below(s)
            ge = gg[k // 4]
            base = lax.rem(k, 4) * 24
            for w in range(4):
                e = pltpu.roll(ge, lax.rem(96 - 6 * w + LANES - base, LANES), 1)
                parts = (
                    pltpu.roll(up, (LANES - WIN * w) % LANES, 1) if w else up,
                    pltpu.roll(s, (LANES + WIN - WIN * w) % LANES, 1) if w != 1 else s,
                    pltpu.roll(dn, (LANES + 2 * WIN - WIN * w) % LANES, 1) if w != 2 else dn,
                    jnp.where(lane < 102, e, 1.0),
                )
                x = quarters(lane, parts).astype(BF)
                at = group * w + ROWS * b
                xs[at : at + ROWS, 0:LANES] = x
                xs[at : at + ROWS, LANES : 2 * LANES] = x
        x = xs[...]
        for n in range(4):
            h = jnp.dot(x, w1_ref[:, 256 * n : 256 * (n + 1)], preferred_element_type=F)
            hs[:, 256 * n : 256 * (n + 1)] = jnp.maximum(h.astype(BF), jnp.zeros((), BF))

        @pl.when(it == 0)
        def _():
            hs[0:ROWS, 0:32] = jnp.zeros((ROWS, 32), BF)

        @pl.when(it == BLOCKS // BPI - 1)
        def _():
            hs[4 * group - ROWS : 4 * group, WIN * 32 - 32 : WIN * 32] = jnp.zeros((ROWS, 32), BF)

        p = [
            jnp.dot(
                hs[group * w : group * (w + 1), :], w2_ref[:, LANES * w : LANES * (w + 1)], preferred_element_type=F
            )
            for w in range(4)
        ]
        for b in range(BPI):
            k = it * BPI + b
            pb = [p[w][ROWS * b : ROWS * (b + 1)] for w in range(4)]
            a0 = quarters(lane, pb)
            a1 = pltpu.roll(quarters(lane, [pb[3], pb[0], pb[1], pb[2]]), LANES - WIN, 1)
            a2 = pltpu.roll(quarters(lane, [pb[2], pb[3], pb[0], pb[1]]), LANES - 2 * WIN, 1)
            acc[k] = a1 + from_above(a0) + from_below(a2)
            base = lax.rem(k, 4) * 24
            tot = ee[k // 4]
            for w in range(4):
                moved = pltpu.roll(pb[w], lax.rem(base + 6 * w + LANES - WIN * ((w + 3) % 4), LANES), 1)
                tot = jnp.where((lane >= base + 6 * w) & (lane < base + 6 * w + 6), moved, tot)
            ee[k // 4] = tot
        return carry

    lax.fori_loop(0, BLOCKS // BPI, step, 0)
    kind = lax.rem(lane, 3)
    his, los = [], []
    for half in range(2):
        hi, lo = settle(kind, ee[half])
        his.append(hi)
        los.append(lo)
    hi = jnp.concatenate(his, axis=1)
    lo = jnp.concatenate(los, axis=1)
    for k in range(0, BLOCKS, 2):
        pick = sel2_ref[:, LANES * k : LANES * (k + 2)]
        extra = jnp.dot(hi, pick, preferred_element_type=F) + jnp.dot(lo, pick, preferred_element_type=F)
        for u in range(2):
            total = acc[k + u] + extra[:, LANES * u : LANES * (u + 1)]
            if k + u == 0:
                part_ref[0] = total
            elif k + u == BLOCKS - 1:
                part_ref[1] = total
            else:
                out_ref[:, LANES * (k + u) : LANES * (k + u + 1)] = total.astype(BF)


def settle(kind, v):
    c = jnp.where(kind == 0, from_above(v), jnp.where(kind == 1, v, from_below(v)))
    hi = c.astype(BF)
    return hi, (c - hi.astype(F)).astype(BF)


def sides_body(
    ends_ref, q_ref, left_ref, right_ref, own_ref, part_ref, w1x_ref, w2x_ref, selx_ref, sel3_ref, old_ref,
    out_ref, held, sems,
):
    del old_ref
    lane = lax.broadcasted_iota(I, (ROWS, LANES), 1)
    edge = jnp.concatenate([left_ref[...], right_ref[...]], axis=0)
    se = lax.dot_general(q_ref[...], edge, NT, preferred_element_type=F).astype(BF).astype(F)
    top = lax.broadcasted_iota(I, (ROWS, 16), 0) < ROWS // 2
    left = lax.broadcasted_iota(I, (ROWS, 16), 1) < 8
    bits = edge.astype(F)
    keep = jnp.where(
        top, jnp.where(left, bits[2:3, 0:1], bits[10:11, 0:1]), jnp.where(left, bits[3:4, 0:1], bits[11:12, 0:1])
    )
    g0 = jnp.where(lane >= 96, own_ref[...], 0.0)
    g0 = g0 + jnp.dot((se * keep).astype(BF), selx_ref[...], preferred_element_type=F)
    g = g0 + pltpu.roll(from_above(g0), LANES - 1, 1) + pltpu.roll(from_below(g0), 1, 1)
    xw = jnp.where((lane >= 120) & (lane < 123), 1.0, g).astype(BF)
    hx = jnp.dot(xw, w1x_ref[0:LANES, :], preferred_element_type=F)
    hx = hx + jnp.dot(xw, w1x_ref[LANES : 2 * LANES, :], preferred_element_type=F)
    live = jnp.where(lane < 32, ends_ref[0], jnp.where(lane >= 96, ends_ref[1], 1))
    hx = jnp.maximum(hx, 0.0) * live.astype(F)
    sums = jnp.dot(hx.astype(BF), w2x_ref[...], preferred_element_type=F)
    hi, lo = settle(lax.rem(lane, 3), sums)
    extra = jnp.dot(hi, sel3_ref[...], preferred_element_type=F) + jnp.dot(lo, sel3_ref[...], preferred_element_type=F)
    copies = []
    for side in range(2):
        held[side] = (part_ref[side] + extra[:, LANES * side : LANES * (side + 1)]).astype(BF)
        block = out_ref.at[:, pl.ds(side * (COLS - LANES), LANES)]
        copies.append(pltpu.make_async_copy(held.at[side], block, sems.at[side]))
        copies[-1].start()
    for copy in copies:
        copy.wait()


def iotas(rows, cols):
    return lax.broadcasted_iota(I, (rows, cols), 0), lax.broadcasted_iota(I, (rows, cols), 1)


def weights(w_first, b_first, w_second):
    coarse = functools.partial(lax.reduce_precision, exponent_bits=8, mantissa_bits=7)
    hi = coarse(w_first)
    mid = w_first - hi
    b0 = coarse(b_first)
    b1 = coarse(b_first - b0)
    b2 = b_first - b0 - b1
    second = w_second.astype(F)
    rows = jnp.concatenate([hi, mid, jnp.stack([b0, b1, b2])])
    wide = jnp.tile(rows, (1, WIN))
    tall = jnp.tile(second.T, (WIN, 1))
    width = WIN * 32
    row, col = iotas(LANES, width)
    pos = col // 32
    shift, inner = row // WIN, row % WIN
    halves = []
    for part in range(2):
        total = jnp.zeros((LANES, width), F)
        for a in range(3):
            for b in range(3):
                tap = wide[9 * part + 3 * a + b][None, :]
                hit = (shift == a) & (inner == pos + b - 1)
                if b == 0:
                    hit = hit | ((row == 96 + a) & (pos == 0))
                if b == 2:
                    hit = hit | ((row == 99 + a) & (pos == WIN - 1))
                total = total + jnp.where(hit, tap, 0.0)
        if part == 0:
            for j in range(3):
                total = total + jnp.where(row == 102 + j, wide[18 + j][None, :], 0.0)
        halves.append(total.astype(BF))
    w1 = jnp.concatenate(halves)
    row, col = iotas(width, 4 * LANES)
    pos = row // 32
    w = col // LANES
    a_of = ((col % LANES) // WIN + 4 - w) % 4
    inner = col % WIN
    total = jnp.zeros((width, 4 * LANES), F)
    for a in range(3):
        for b in range(3):
            hit = (a_of == a) & (inner == pos + 1 - b)
            if b == 2:
                hit = hit | ((a_of == 3) & (inner == a) & (pos == 0))
            if b == 0:
                hit = hit | ((a_of == 3) & (inner == 3 + a) & (pos == WIN - 1))
            total = total + jnp.where(hit, tall[:, 3 * a + b][:, None], 0.0)
    w2 = total.astype(BF)
    row, col = iotas(LANES, LANES)
    halves = []
    for part in range(2):
        total = jnp.zeros((LANES, LANES), F)
        for a in range(3):
            for b in range(3):
                tap = wide[9 * part + 3 * a + b, :LANES][None, :]
                hit = jnp.zeros((LANES, LANES), jnp.bool_)
                for h in range(4):
                    hit = hit | ((col // 32 == h) & (row == SIDE_LANE[SIDE_HIDDEN[h] + b - 1] - 1 + a))
                total = total + jnp.where(hit, tap, 0.0)
        if part == 0:
            for j in range(3):
                total = total + jnp.where(row == 120 + j, wide[18 + j, :LANES][None, :], 0.0)
        halves.append(total.astype(BF))
    w1x = jnp.concatenate(halves)
    total = jnp.zeros((LANES, LANES), F)
    for a in range(3):
        for b in range(3):
            hit = jnp.zeros((LANES, LANES), jnp.bool_)
            for h in range(4):
                for j, out in enumerate((0, 1, COLS - 2, COLS - 1)):
                    if SIDE_HIDDEN[h] == out + b - 1:
                        hit = hit | ((row // 32 == h) & (col == 3 * j + a))
            total = total + jnp.where(hit, tall[:LANES, 3 * a + b][:, None], 0.0)
    return w1, w2, w1x, total.astype(BF)


SIDE_LANE = {0: 97, 1: 100, COLS - 2: 103, COLS - 1: 106, -2: 109, -1: 112, COLS: 115, COLS + 1: 118}
SIDE_HIDDEN = (-1, 0, COLS - 1, COLS)


def selectors():
    i, l = np.indices((COLS, 2 * LANES))
    m, s = 16 * (l // LANES) + (l % LANES) // 6, (l % LANES) % 6
    fit = l % LANES < 96
    hit = (fit & (s == 1) & (i == WIN * m - 1)) | (fit & (s == 4) & (i == WIN * m + WIN))
    for c in (0, 1, COLS - 2, COLS - 1):
        hit = hit | ((l == SIDE_LANE[c]) & (i == c))
    sel1 = hit.astype(BF)
    i, l = np.indices((16, LANES))
    hit = np.zeros((16, LANES), bool)
    for row, c in ((0, -2), (1, -1), (8, COLS), (9, COLS + 1)):
        hit = hit | ((i == row) & (l == SIDE_LANE[c]))
    selx = hit.astype(BF)
    l, j = np.indices((2 * LANES, COLS))
    m, s = 16 * (l // LANES) + (l % LANES) // 6, (l % LANES) % 6
    fit = l % LANES < 96
    sel2 = ((fit & (s < 3) & (j == WIN * m - 1)) | (fit & (s >= 3) & (j == WIN * m + WIN))).astype(BF)
    l, j = np.indices((LANES, 2 * LANES))
    hit = np.zeros((LANES, 2 * LANES), bool)
    for n, c in enumerate((0, 1, 2 * LANES - 2, 2 * LANES - 1)):
        hit = hit | ((l // 3 == n) & (j == c))
    return sel1, sel2, selx, hit.astype(BF)


def refine(mask, queries, slab, tables):
    vmem = pl.BlockSpec(memory_space=pltpu.VMEM)
    hbm = pl.BlockSpec(memory_space=pltpu.HBM)
    arrays = (queries,) + tables
    return pl.pallas_call(
        refine_body,
        out_shape=(
            jax.ShapeDtypeStruct((ROWS, COLS), BF),
            jax.ShapeDtypeStruct((ROWS, LANES), F),
            jax.ShapeDtypeStruct((2, ROWS, LANES), F),
        ),
        in_specs=[pl.BlockSpec(memory_space=pltpu.SMEM), vmem] + [hbm] * len(arrays),
        out_specs=(vmem, vmem, vmem),
        scratch_shapes=[
            pltpu.VMEM((BLOCKS, ROWS, LANES), F),
            pltpu.VMEM((2, ROWS, LANES), F),
            pltpu.VMEM((4 * ROWS * BPI, 2 * LANES), BF),
            pltpu.VMEM((4 * ROWS * BPI, WIN * 32), BF),
            pltpu.VMEM((BLOCKS, ROWS, LANES), F),
            pltpu.VMEM((2, ROWS, LANES), F),
        ]
        + [pltpu.VMEM(array.shape, BF) for array in arrays]
        + [pltpu.SemaphoreType.DMA((len(arrays),))],
        compiler_params=pltpu.CompilerParams(vmem_limit_bytes=36 * 1024 * 1024),
        cost_estimate=pl.CostEstimate(flops=9_400_000_000, bytes_accessed=8_000_000, transcendentals=0),
        name="refine",
    )(mask, slab, *arrays)


def sides(ends, queries, left, right, own, part, tables, out):
    vmem = pl.BlockSpec(memory_space=pltpu.VMEM)
    any_space = pl.BlockSpec(memory_space=pl.ANY)
    return pl.pallas_call(
        sides_body,
        out_shape=jax.ShapeDtypeStruct((ROWS, COLS), BF),
        in_specs=[pl.BlockSpec(memory_space=pltpu.SMEM)] + [vmem] * 9 + [any_space],
        out_specs=any_space,
        scratch_shapes=[pltpu.VMEM((2, ROWS, LANES), BF), pltpu.SemaphoreType.DMA((2,))],
        input_output_aliases={10: 0},
        compiler_params=pltpu.CompilerParams(vmem_limit_bytes=8 * 1024 * 1024),
        cost_estimate=pl.CostEstimate(flops=60_000_000, bytes_accessed=1_500_000, transcendentals=0),
        name="sides",
    )(ends, queries, left, right, own, part, *tables, out)


def pack_body(me_ref, time_ref, panels_ref, out_ref, sems):
    me = me_ref[0]
    first = me - lax.rem(me, 2)
    jobs = []
    for i in range(2 * BLOCKS):
        owner = time_ref[first * BLOCKS + i] // BLOCKS
        slot = owner - lax.rem(owner, 2) + i // BLOCKS
        copy = pltpu.make_async_copy(panels_ref.at[i], out_ref.at[slot], sems.at[i])
        jobs.append((lax.rem(owner, 2) == lax.rem(me, 2), copy))
    for wanted, copy in jobs:
        pl.when(wanted)(copy.start)
    for wanted, copy in jobs:
        pl.when(wanted)(copy.wait)


def pack(me, panel_time, panels, owners):
    any_space = pl.BlockSpec(memory_space=pl.ANY)
    smem = pl.BlockSpec(memory_space=pltpu.SMEM)
    return pl.pallas_call(
        pack_body,
        out_shape=jax.ShapeDtypeStruct((owners,) + panels.shape[1:], BF),
        in_specs=[smem, smem, any_space],
        out_specs=any_space,
        scratch_shapes=[pltpu.SemaphoreType.DMA((2 * BLOCKS,))],
        compiler_params=pltpu.CompilerParams(vmem_limit_bytes=4 * 1024 * 1024),
        cost_estimate=pl.CostEstimate(flops=0, bytes_accessed=600_000, transcendentals=0),
        name="pack",
    )(me, panel_time, panels)


def place_body(source_ref, incoming_ref, *rest):
    out_ref, held, in_sems, out_sems = rest[-4:]
    gets = [
        pltpu.make_async_copy(incoming_ref.at[source_ref[k]], held.at[k], in_sems.at[k]) for k in range(BLOCKS)
    ]
    for copy in gets:
        copy.start()
    for copy in gets:
        copy.wait()
    puts = [pltpu.make_async_copy(held, out_ref.at[d], out_sems.at[d]) for d in range(out_ref.shape[0])]
    for copy in puts:
        copy.start()
    for copy in puts:
        copy.wait()


def place(source, incoming, copies, ready):
    any_space = pl.BlockSpec(memory_space=pl.ANY)
    piece = incoming.shape[1:]
    return pl.pallas_call(
        place_body,
        out_shape=jax.ShapeDtypeStruct((copies, BLOCKS) + piece, BF),
        in_specs=[pl.BlockSpec(memory_space=pltpu.SMEM)] + [any_space] * (1 + len(ready)),
        out_specs=any_space,
        scratch_shapes=[
            pltpu.VMEM((BLOCKS,) + piece, BF),
            pltpu.SemaphoreType.DMA((BLOCKS,)),
            pltpu.SemaphoreType.DMA((copies,)),
        ],
        compiler_params=pltpu.CompilerParams(vmem_limit_bytes=4 * 1024 * 1024),
        cost_estimate=pl.CostEstimate(flops=0, bytes_accessed=2_400_000, transcendentals=0),
        name="place",
    )(source, incoming, *ready)


def shards(queries, ref_panels, cand_mask, panel_time, w_first, b_first, w_second):
    owners = lax.axis_size("ref")
    fan = lax.axis_size("qry")
    me = lax.axis_index("ref")
    up = [(i, i + 1) for i in range(owners - 1)]
    down = [(i + 1, i) for i in range(owners - 1)]
    pairs = [[2 * z, 2 * z + 1] for z in range(owners // 2)]
    lines = [[2 * z + c for z in range(owners // 2)] for c in range(2)]
    chip = lax.all_gather(ref_panels, "ref", axis=0, tiled=True, axis_index_groups=pairs)
    packed = pack(me[None], panel_time, chip, owners)
    incoming = lax.all_to_all(packed, "ref", 0, 0, tiled=True, axis_index_groups=lines)

    holder = jnp.arange(owners * BLOCKS, dtype=I) // BLOCKS
    mine = panel_time[None, :] == me * BLOCKS + jnp.arange(BLOCKS, dtype=I)[:, None]
    source = jnp.sum(jnp.where(mine, holder[None, :], 0), axis=1)
    ends = jnp.stack([(me > 0).astype(I), (me < owners - 1).astype(I)])
    w1, w2, w1x, w2x = weights(w_first, b_first, w_second)
    sel1, sel2, selx, sel3 = selectors()

    marks = [
        jnp.broadcast_to(cand_mask[:, c : c + 1].astype(BF)[None], (3, 2, queries.shape[1])).reshape(6, -1)
        for c in (0, BLOCKS - 1)
    ]
    ready = (w1, w2, w1x, w2x, ends) + tuple(marks)
    slab = lax.all_to_all(place(source, incoming, fan, ready), "qry", 0, 0, tiled=True)
    head = jnp.concatenate([slab[0, 0, 0:2], marks[0]])
    tail = jnp.concatenate([slab[fan - 1, BLOCKS - 1, 6:8], marks[1]])
    from_left = lax.ppermute(tail, "ref", up)
    from_right = lax.ppermute(head, "ref", down)
    out, own, part = refine(cand_mask, queries, slab, (sel1, w1, w2, sel2))
    return sides(ends, queries, from_left, from_right, own, part, (w1x, w2x, selx, sel3), out)


def solution(mesh):
    placed = (P("qry", None), P("ref", "qry", None), P("qry", "ref"), P(), P(), P(), P())
    return jax.shard_map(
        shards, mesh=mesh, in_specs=placed, out_specs=P("qry", "ref"), check_vma=False
    )
```

```python
import functools

import jax
import jax.numpy as jnp
import numpy as np
from jax import lax
from jax.experimental import pallas as pl
from jax.experimental.pallas import tpu as pltpu
from jax.sharding import PartitionSpec as P

BF = jnp.bfloat16
F = jnp.float32
I = jnp.int32
NT = (((1,), (1,)), ((), ()))
ROWS = 256
COLS = 1024
BLOCKS = 8
LANES = 128
WIN = 32
BPI = 4


def from_above(v):
    row = lax.broadcasted_iota(I, v.shape, 0)
    return jnp.where(row == 0, 0.0, pltpu.roll(v, 1, 0))


def from_below(v):
    row = lax.broadcasted_iota(I, v.shape, 0)
    n = v.shape[0]
    return jnp.where(row == n - 1, 0.0, pltpu.roll(v, n - 1, 0))


def quarters(lane, four):
    return jnp.where(
        lane < 64,
        jnp.where(lane < 32, four[0], four[1]),
        jnp.where(lane < 96, four[2], four[3]),
    )


def refine_body(
    mask_ref, score_ref, sel1_hbm, w1_hbm, w2_hbm, sel2_hbm,
    out_ref, own_ref, part_ref, sims, gg, xs, hs, acc, ee, sel1_ref, w1_ref, w2_ref, sel2_ref, sems,
):
    loads = [
        pltpu.make_async_copy(src, dst, sems.at[n])
        for n, (src, dst) in enumerate(
            zip((sel1_hbm, w1_hbm, w2_hbm, sel2_hbm), (sel1_ref, w1_ref, w2_ref, sel2_ref))
        )
    ]
    for load in loads:
        load.start()
    lane = lax.broadcasted_iota(I, (ROWS, LANES), 1)
    top = lax.broadcasted_iota(I, (ROWS, LANES), 0) < ROWS // 2
    keep = []
    for half in range(2):
        rows = [quarters(lane, [mask_ref[r, 4 * half + j] for j in range(4)]) for r in range(2)]
        keep.append(jnp.where(top, rows[0], rows[1]).astype(F))
    loads[0].wait()
    g0 = jnp.zeros((ROWS, 2 * LANES), F)
    for n in range(BLOCKS):
        half = n % 2
        v = score_ref[n // 2, :, LANES * half : LANES * (half + 1)].astype(F) * keep[half]
        sims[n] = v
        g0 = g0 + jnp.dot(v.astype(BF), sel1_ref[LANES * n : LANES * (n + 1), :], preferred_element_type=F)
    own_ref[...] = g0[:, :LANES]
    g = g0 + pltpu.roll(from_above(g0), 2 * LANES - 1, 1) + pltpu.roll(from_below(g0), 1, 1)
    gg[0] = g[:, :LANES]
    gg[1] = g[:, LANES:]
    group = ROWS * BPI
    for load in loads[1:]:
        load.wait()

    def step(it, carry):
        ge = gg[it]
        for w in range(4):
            s = sims[2 * w + it]
            up = from_above(s)
            dn = from_below(s)
            for b in range(BPI):
                e = pltpu.roll(ge, (96 - 6 * (4 * b + w)) % LANES, 1)
                parts = (
                    pltpu.roll(up, (LANES - WIN * b) % LANES, 1) if b else up,
                    pltpu.roll(s, (LANES + WIN - WIN * b) % LANES, 1) if b != 1 else s,
                    pltpu.roll(dn, (LANES + 2 * WIN - WIN * b) % LANES, 1) if b != 2 else dn,
                    jnp.where(lane < 102, e, 1.0),
                )
                x = quarters(lane, parts).astype(BF)
                at = group * w + ROWS * b
                xs[at : at + ROWS, 0:LANES] = x
                xs[at : at + ROWS, LANES : 2 * LANES] = x
        x = xs[...]
        for n in range(4):
            h = jnp.dot(x, w1_ref[:, 256 * n : 256 * (n + 1)], preferred_element_type=F)
            hs[:, 256 * n : 256 * (n + 1)] = jnp.maximum(h.astype(BF), jnp.zeros((), BF))

        @pl.when(it == 0)
        def _():
            hs[0:ROWS, 0:32] = jnp.zeros((ROWS, 32), BF)

        @pl.when(it == BLOCKS // BPI - 1)
        def _():
            hs[4 * group - ROWS : 4 * group, WIN * 32 - 32 : WIN * 32] = jnp.zeros((ROWS, 32), BF)

        p = [
            jnp.dot(
                hs[group * w : group * (w + 1), :], w2_ref[:, LANES * w : LANES * (w + 1)], preferred_element_type=F
            )
            for w in range(4)
        ]
        tot = jnp.zeros((ROWS, LANES), F)
        for b in range(BPI):
            k = it * BPI + b
            pb = [p[w][ROWS * b : ROWS * (b + 1)] for w in range(4)]
            a0 = quarters(lane, pb)
            a1 = pltpu.roll(quarters(lane, [pb[3], pb[0], pb[1], pb[2]]), LANES - WIN, 1)
            a2 = pltpu.roll(quarters(lane, [pb[2], pb[3], pb[0], pb[1]]), LANES - 2 * WIN, 1)
            acc[k] = a1 + from_above(a0) + from_below(a2)
            for w in range(4):
                at = 6 * (4 * b + w)
                moved = pltpu.roll(pb[w], (at + LANES - WIN * ((w + 3) % 4)) % LANES, 1)
                tot = jnp.where((lane >= at) & (lane < at + 6), moved, tot)
        ee[it] = tot
        return carry

    lax.fori_loop(0, BLOCKS // BPI, step, 0)
    kind = lax.rem(lane, 3)
    his, los = [], []
    for half in range(2):
        hi, lo = settle(kind, ee[half])
        his.append(hi)
        los.append(lo)
    hi = jnp.concatenate(his, axis=1)
    lo = jnp.concatenate(los, axis=1)
    for k in range(0, BLOCKS, 2):
        pick = sel2_ref[:, LANES * k : LANES * (k + 2)]
        extra = jnp.dot(hi, pick, preferred_element_type=F) + jnp.dot(lo, pick, preferred_element_type=F)
        for u in range(2):
            total = acc[k + u] + extra[:, LANES * u : LANES * (u + 1)]
            if k + u == 0:
                part_ref[0] = total
            elif k + u == BLOCKS - 1:
                part_ref[1] = total
            else:
                out_ref[:, LANES * (k + u) : LANES * (k + u + 1)] = total.astype(BF)


def settle(kind, v):
    c = jnp.where(kind == 0, from_above(v), jnp.where(kind == 1, v, from_below(v)))
    hi = c.astype(BF)
    return hi, (c - hi.astype(F)).astype(BF)


def sides_body(
    ends_ref, left_ref, right_ref, own_ref, part_ref, w1x_ref, w2x_ref, selx_ref, sel3_ref, old_ref,
    out_ref, held, sems,
):
    del old_ref
    lane = lax.broadcasted_iota(I, (ROWS, LANES), 1)
    near = jnp.concatenate([left_ref[...], right_ref[...]], axis=1)
    g0 = jnp.where(lane >= 96, own_ref[...], 0.0) + jnp.dot(near, selx_ref[...], preferred_element_type=F)
    g = g0 + pltpu.roll(from_above(g0), LANES - 1, 1) + pltpu.roll(from_below(g0), 1, 1)
    xw = jnp.where((lane >= 120) & (lane < 123), 1.0, g).astype(BF)
    hx = jnp.dot(xw, w1x_ref[0:LANES, :], preferred_element_type=F)
    hx = hx + jnp.dot(xw, w1x_ref[LANES : 2 * LANES, :], preferred_element_type=F)
    live = jnp.where(lane < 32, ends_ref[0], jnp.where(lane >= 96, ends_ref[1], 1))
    hx = jnp.maximum(hx, 0.0) * live.astype(F)
    sums = jnp.dot(hx.astype(BF), w2x_ref[...], preferred_element_type=F)
    hi, lo = settle(lax.rem(lane, 3), sums)
    extra = jnp.dot(hi, sel3_ref[...], preferred_element_type=F) + jnp.dot(lo, sel3_ref[...], preferred_element_type=F)
    copies = []
    for side in range(2):
        held[side] = (part_ref[side] + extra[:, LANES * side : LANES * (side + 1)]).astype(BF)
        block = out_ref.at[:, pl.ds(side * (COLS - LANES), LANES)]
        copies.append(pltpu.make_async_copy(held.at[side], block, sems.at[side]))
        copies[-1].start()
    for copy in copies:
        copy.wait()


def iotas(rows, cols):
    return lax.broadcasted_iota(I, (rows, cols), 0), lax.broadcasted_iota(I, (rows, cols), 1)


def weights(w_first, b_first, w_second):
    coarse = functools.partial(lax.reduce_precision, exponent_bits=8, mantissa_bits=7)
    hi = coarse(w_first)
    mid = w_first - hi
    b0 = coarse(b_first)
    b1 = coarse(b_first - b0)
    b2 = b_first - b0 - b1
    second = w_second.astype(F)
    rows = jnp.concatenate([hi, mid, jnp.stack([b0, b1, b2])])
    wide = jnp.tile(rows, (1, WIN))
    tall = jnp.tile(second.T, (WIN, 1))
    width = WIN * 32
    row, col = iotas(LANES, width)
    pos = col // 32
    shift, inner = row // WIN, row % WIN
    halves = []
    for part in range(2):
        total = jnp.zeros((LANES, width), F)
        for a in range(3):
            for b in range(3):
                tap = wide[9 * part + 3 * a + b][None, :]
                hit = (shift == a) & (inner == pos + b - 1)
                if b == 0:
                    hit = hit | ((row == 96 + a) & (pos == 0))
                if b == 2:
                    hit = hit | ((row == 99 + a) & (pos == WIN - 1))
                total = total + jnp.where(hit, tap, 0.0)
        if part == 0:
            for j in range(3):
                total = total + jnp.where(row == 102 + j, wide[18 + j][None, :], 0.0)
        halves.append(total.astype(BF))
    w1 = jnp.concatenate(halves)
    row, col = iotas(width, 4 * LANES)
    pos = row // 32
    w = col // LANES
    a_of = ((col % LANES) // WIN + 4 - w) % 4
    inner = col % WIN
    total = jnp.zeros((width, 4 * LANES), F)
    for a in range(3):
        for b in range(3):
            hit = (a_of == a) & (inner == pos + 1 - b)
            if b == 2:
                hit = hit | ((a_of == 3) & (inner == a) & (pos == 0))
            if b == 0:
                hit = hit | ((a_of == 3) & (inner == 3 + a) & (pos == WIN - 1))
            total = total + jnp.where(hit, tall[:, 3 * a + b][:, None], 0.0)
    w2 = total.astype(BF)
    row, col = iotas(LANES, LANES)
    halves = []
    for part in range(2):
        total = jnp.zeros((LANES, LANES), F)
        for a in range(3):
            for b in range(3):
                tap = wide[9 * part + 3 * a + b, :LANES][None, :]
                hit = jnp.zeros((LANES, LANES), jnp.bool_)
                for h in range(4):
                    hit = hit | ((col // 32 == h) & (row == SIDE_LANE[SIDE_HIDDEN[h] + b - 1] - 1 + a))
                total = total + jnp.where(hit, tap, 0.0)
        if part == 0:
            for j in range(3):
                total = total + jnp.where(row == 120 + j, wide[18 + j, :LANES][None, :], 0.0)
        halves.append(total.astype(BF))
    w1x = jnp.concatenate(halves)
    total = jnp.zeros((LANES, LANES), F)
    for a in range(3):
        for b in range(3):
            hit = jnp.zeros((LANES, LANES), jnp.bool_)
            for h in range(4):
                for j, out in enumerate((0, 1, COLS - 2, COLS - 1)):
                    if SIDE_HIDDEN[h] == out + b - 1:
                        hit = hit | ((row // 32 == h) & (col == 3 * j + a))
            total = total + jnp.where(hit, tall[:LANES, 3 * a + b][:, None], 0.0)
    return w1, w2, w1x, total.astype(BF)


SIDE_LANE = {0: 97, 1: 100, COLS - 2: 103, COLS - 1: 106, -2: 109, -1: 112, COLS: 115, COLS + 1: 118}
SIDE_HIDDEN = (-1, 0, COLS - 1, COLS)


def selectors():
    i, l = np.indices((COLS, 2 * LANES))
    i = i % WIN + WIN * (i // (BLOCKS * WIN)) + LANES * (i // WIN % BLOCKS)
    m, s = 16 * (l // LANES) + (l % LANES) // 6, (l % LANES) % 6
    fit = l % LANES < 96
    hit = (fit & (s == 1) & (i == WIN * m - 1)) | (fit & (s == 4) & (i == WIN * m + WIN))
    for c in (0, 1, COLS - 2, COLS - 1):
        hit = hit | ((l == SIDE_LANE[c]) & (i == c))
    sel1 = hit.astype(BF)
    i, l = np.indices((2 * LANES, LANES))
    hit = np.zeros((2 * LANES, LANES), bool)
    for row, c in ((LANES - 2, -2), (LANES - 1, -1), (LANES, COLS), (LANES + 1, COLS + 1)):
        hit = hit | ((i == row) & (l == SIDE_LANE[c]))
    selx = hit.astype(BF)
    l, j = np.indices((2 * LANES, COLS))
    m, s = 16 * (l // LANES) + (l % LANES) // 6, (l % LANES) % 6
    fit = l % LANES < 96
    sel2 = ((fit & (s < 3) & (j == WIN * m - 1)) | (fit & (s >= 3) & (j == WIN * m + WIN))).astype(BF)
    l, j = np.indices((LANES, 2 * LANES))
    hit = np.zeros((LANES, 2 * LANES), bool)
    for n, c in enumerate((0, 1, 2 * LANES - 2, 2 * LANES - 1)):
        hit = hit | ((l // 3 == n) & (j == c))
    return sel1, sel2, selx, hit.astype(BF)


def refine(mask, scores, tables):
    vmem = pl.BlockSpec(memory_space=pltpu.VMEM)
    hbm = pl.BlockSpec(memory_space=pltpu.HBM)
    arrays = tables
    return pl.pallas_call(
        refine_body,
        out_shape=(
            jax.ShapeDtypeStruct((ROWS, COLS), BF),
            jax.ShapeDtypeStruct((ROWS, LANES), F),
            jax.ShapeDtypeStruct((2, ROWS, LANES), F),
        ),
        in_specs=[pl.BlockSpec(memory_space=pltpu.SMEM), vmem] + [hbm] * len(arrays),
        out_specs=(vmem, vmem, vmem),
        scratch_shapes=[
            pltpu.VMEM((BLOCKS, ROWS, LANES), F),
            pltpu.VMEM((2, ROWS, LANES), F),
            pltpu.VMEM((4 * ROWS * BPI, 2 * LANES), BF),
            pltpu.VMEM((4 * ROWS * BPI, WIN * 32), BF),
            pltpu.VMEM((BLOCKS, ROWS, LANES), F),
            pltpu.VMEM((2, ROWS, LANES), F),
        ]
        + [pltpu.VMEM(array.shape, BF) for array in arrays]
        + [pltpu.SemaphoreType.DMA((len(arrays),))],
        compiler_params=pltpu.CompilerParams(vmem_limit_bytes=36 * 1024 * 1024),
        cost_estimate=pl.CostEstimate(flops=9_400_000_000, bytes_accessed=8_000_000, transcendentals=0),
        name="refine",
    )(mask, scores, *arrays)


def sides(ends, left, right, own, part, tables, out):
    vmem = pl.BlockSpec(memory_space=pltpu.VMEM)
    any_space = pl.BlockSpec(memory_space=pl.ANY)
    return pl.pallas_call(
        sides_body,
        out_shape=jax.ShapeDtypeStruct((ROWS, COLS), BF),
        in_specs=[pl.BlockSpec(memory_space=pltpu.SMEM)] + [vmem] * 8 + [any_space],
        out_specs=any_space,
        scratch_shapes=[pltpu.VMEM((2, ROWS, LANES), BF), pltpu.SemaphoreType.DMA((2,))],
        input_output_aliases={9: 0},
        compiler_params=pltpu.CompilerParams(vmem_limit_bytes=8 * 1024 * 1024),
        cost_estimate=pl.CostEstimate(flops=60_000_000, bytes_accessed=1_500_000, transcendentals=0),
        name="sides",
    )(ends, left, right, own, part, *tables, out)


def score_body(seat_ref, slab_ref, *rest):
    q_refs, out_ref = rest[:-1], rest[-1]
    side = len(q_refs)
    slab = slab_ref[...].swapaxes(0, 1).reshape(BLOCKS * WIN, slab_ref.shape[3])
    for step, q_ref in enumerate(q_refs):
        v = lax.rem(seat_ref[0] + side - step, side)
        out_ref[v] = lax.dot_general(q_ref[...], slab, NT, preferred_element_type=F).astype(BF)


def score(seat, slab, videos):
    vmem = pl.BlockSpec(memory_space=pltpu.VMEM)
    return pl.pallas_call(
        score_body,
        out_shape=jax.ShapeDtypeStruct((len(videos), ROWS, BLOCKS * WIN), BF),
        in_specs=[pl.BlockSpec(memory_space=pltpu.SMEM), vmem] + [vmem] * len(videos),
        out_specs=vmem,
        compiler_params=pltpu.CompilerParams(vmem_limit_bytes=12 * 1024 * 1024),
        cost_estimate=pl.CostEstimate(flops=540_000_000, bytes_accessed=3_100_000, transcendentals=0),
        name="score",
    )(seat, slab, *videos)


def pack_body(me_ref, time_ref, panels_ref, out_ref, zero_ref, sems):
    me = me_ref[0]
    first = me - lax.rem(me, 2)
    jobs = []
    for i in range(2 * BLOCKS):
        owner = time_ref[first * BLOCKS + i] // BLOCKS
        slot = owner - lax.rem(owner, 2) + i // BLOCKS
        copy = pltpu.make_async_copy(panels_ref.at[i], out_ref.at[slot], sems.at[i])
        jobs.append((lax.rem(owner, 2) == lax.rem(me, 2), copy))
    for wanted, copy in jobs:
        pl.when(wanted)(copy.start)
    zero_ref[...] = jnp.zeros(zero_ref.shape, F)
    for wanted, copy in jobs:
        pl.when(wanted)(copy.wait)


def pack(me, panel_time, panels, owners):
    any_space = pl.BlockSpec(memory_space=pl.ANY)
    smem = pl.BlockSpec(memory_space=pltpu.SMEM)
    return pl.pallas_call(
        pack_body,
        out_shape=(
            jax.ShapeDtypeStruct((owners,) + panels.shape[1:], BF),
            jax.ShapeDtypeStruct((8, LANES), F),
        ),
        in_specs=[smem, smem, any_space],
        out_specs=(any_space, pl.BlockSpec(memory_space=pltpu.VMEM)),
        scratch_shapes=[pltpu.SemaphoreType.DMA((2 * BLOCKS,))],
        compiler_params=pltpu.CompilerParams(vmem_limit_bytes=4 * 1024 * 1024),
        cost_estimate=pl.CostEstimate(flops=0, bytes_accessed=600_000, transcendentals=0),
        name="pack",
    )(me, panel_time, panels)


def share_body(q_ref, *rest):
    out_ref = rest[-1]
    out_ref[...] = q_ref[...]


def share(queries, after):
    vmem = pl.BlockSpec(memory_space=pltpu.VMEM)
    return pl.pallas_call(
        share_body,
        out_shape=jax.ShapeDtypeStruct(queries.shape, BF),
        in_specs=[vmem] + [pl.BlockSpec(memory_space=pl.ANY)] * len(after),
        out_specs=vmem,
        compiler_params=pltpu.CompilerParams(vmem_limit_bytes=4 * 1024 * 1024),
        cost_estimate=pl.CostEstimate(flops=0, bytes_accessed=1_000_000, transcendentals=0),
        name="share",
    )(queries, *after)


def place_body(source_ref, incoming_ref, *rest):
    out_ref, held, in_sems, out_sems = rest[-4:]
    gets = [
        pltpu.make_async_copy(incoming_ref.at[source_ref[k]], held.at[k], in_sems.at[k]) for k in range(BLOCKS)
    ]
    for copy in gets:
        copy.start()
    for copy in gets:
        copy.wait()
    puts = [pltpu.make_async_copy(held, out_ref.at[d], out_sems.at[d]) for d in range(out_ref.shape[0])]
    for copy in puts:
        copy.start()
    for copy in puts:
        copy.wait()


def place(source, incoming, copies, ready):
    any_space = pl.BlockSpec(memory_space=pl.ANY)
    piece = incoming.shape[1:]
    return pl.pallas_call(
        place_body,
        out_shape=jax.ShapeDtypeStruct((copies, BLOCKS) + piece, BF),
        in_specs=[pl.BlockSpec(memory_space=pltpu.SMEM)] + [any_space] * (1 + len(ready)),
        out_specs=any_space,
        scratch_shapes=[
            pltpu.VMEM((BLOCKS,) + piece, BF),
            pltpu.SemaphoreType.DMA((BLOCKS,)),
            pltpu.SemaphoreType.DMA((copies,)),
        ],
        compiler_params=pltpu.CompilerParams(vmem_limit_bytes=4 * 1024 * 1024),
        cost_estimate=pl.CostEstimate(flops=0, bytes_accessed=400_000_000, transcendentals=0),
        name="place",
    )(source, incoming, *ready)


def shards(queries, ref_panels, cand_mask, panel_time, w_first, b_first, w_second):
    owners = lax.axis_size("ref")
    fan = lax.axis_size("qry")
    me = lax.axis_index("ref")
    up = [(i, i + 1) for i in range(owners - 1)]
    down = [(i + 1, i) for i in range(owners - 1)]
    pairs = [[2 * z, 2 * z + 1] for z in range(owners // 2)]
    lines = [[2 * z + c for z in range(owners // 2)] for c in range(2)]
    side = LANES // WIN
    outer = [[i + side * j for j in range(side)] for i in range(fan // side)]
    inner = [[side * j + i for i in range(side)] for j in range(fan // side)]
    chip = lax.all_gather(ref_panels, "ref", axis=0, tiled=True, axis_index_groups=pairs)
    packed, zero = pack(me[None], panel_time, chip, owners)
    incoming = lax.all_to_all(packed, "ref", 0, 0, tiled=True, axis_index_groups=lines)
    holder = jnp.arange(owners * BLOCKS, dtype=I) // BLOCKS
    mine = panel_time[None, :] == me * BLOCKS + jnp.arange(BLOCKS, dtype=I)[:, None]
    source = jnp.sum(jnp.where(mine, holder[None, :], 0), axis=1)
    ends = jnp.stack([(me > 0).astype(I), (me < owners - 1).astype(I)])
    w1, w2, w1x, w2x = weights(w_first, b_first, w_second)
    sel1, sel2, selx, sel3 = selectors()

    shared = share(queries, (zero, w1, w2, w1x, w2x))
    videos = [shared] + [
        lax.ppermute(
            shared, "qry", [(g[i], g[(i + step) % side]) for g in outer for i in range(side)]
        )
        for step in range(1, side)
    ]
    seat = lax.axis_index("qry") // (fan // side)

    rows = [jnp.repeat(cand_mask[:, c].astype(BF), ROWS // 2)[:, None] for c in (0, BLOCKS - 1)]
    ready = (w1, w2, w1x, w2x, ends) + tuple(rows)
    slab = lax.all_to_all(
        place(source, incoming, side, ready), "qry", 0, 0, tiled=True, axis_index_groups=inner
    )
    scores = lax.all_to_all(score(seat[None], slab, videos), "qry", 0, 0, tiled=True, axis_index_groups=outer)
    head = scores[0, :, :LANES] * rows[0]
    tail = scores[side - 1, :, LANES:] * rows[1]
    from_left = lax.ppermute(tail, "ref", up)
    from_right = lax.ppermute(head, "ref", down)
    out, own, part = refine(cand_mask, scores, (sel1, w1, w2, sel2))
    return sides(ends, from_left, from_right, own, part, (w1x, w2x, selx, sel3), out)


def solution(mesh):
    placed = (P("qry", None), P("ref", "qry", None), P("qry", "ref"), P(), P(), P(), P())
    return jax.shard_map(
        shards, mesh=mesh, in_specs=placed, out_specs=P("qry", "ref"), check_vma=False
    )
```

```python
import functools

import jax
import jax.numpy as jnp
import numpy as np
from jax import lax
from jax.experimental import pallas as pl
from jax.experimental.pallas import tpu as pltpu
from jax.sharding import PartitionSpec as P

BF = jnp.bfloat16
F = jnp.float32
I = jnp.int32
NT = (((1,), (1,)), ((), ()))
ROWS = 256
COLS = 1024
BLOCKS = 8
LANES = 128
WIN = 32
BPI = 4


def from_above(v):
    row = lax.broadcasted_iota(I, v.shape, 0)
    return jnp.where(row == 0, 0.0, pltpu.roll(v, 1, 0))


def from_below(v):
    row = lax.broadcasted_iota(I, v.shape, 0)
    n = v.shape[0]
    return jnp.where(row == n - 1, 0.0, pltpu.roll(v, n - 1, 0))


def quarters(lane, four):
    return jnp.where(
        lane < 64,
        jnp.where(lane < 32, four[0], four[1]),
        jnp.where(lane < 96, four[2], four[3]),
    )


def refine_body(
    mask_ref, score_ref, sel1_hbm, w1_hbm, w2_hbm, sel2_hbm,
    out_ref, own_ref, part_ref, sims, gg, xs, hs, acc, ee, sel1_ref, w1_ref, w2_ref, sel2_ref, sems,
):
    loads = [
        pltpu.make_async_copy(src, dst, sems.at[n])
        for n, (src, dst) in enumerate(
            zip((sel1_hbm, w1_hbm, w2_hbm, sel2_hbm), (sel1_ref, w1_ref, w2_ref, sel2_ref))
        )
    ]
    for load in loads:
        load.start()
    lane = lax.broadcasted_iota(I, (ROWS, LANES), 1)
    top = lax.broadcasted_iota(I, (ROWS, LANES), 0) < ROWS // 2
    keep = []
    for half in range(2):
        rows = [quarters(lane, [mask_ref[r, 4 * half + j] for j in range(4)]) for r in range(2)]
        keep.append(jnp.where(top, rows[0], rows[1]).astype(F))
    loads[0].wait()
    g0 = jnp.zeros((ROWS, 2 * LANES), F)
    for n in range(BLOCKS):
        half = n % 2
        v = score_ref[n // 2, :, LANES * half : LANES * (half + 1)].astype(F) * keep[half]
        sims[n] = v
        g0 = g0 + jnp.dot(v.astype(BF), sel1_ref[LANES * n : LANES * (n + 1), :], preferred_element_type=F)
    own_ref[...] = g0[:, :LANES]
    g = g0 + pltpu.roll(from_above(g0), 2 * LANES - 1, 1) + pltpu.roll(from_below(g0), 1, 1)
    gg[0] = g[:, :LANES]
    gg[1] = g[:, LANES:]
    group = ROWS * BPI
    for load in loads[1:]:
        load.wait()

    def step(it, carry):
        ge = gg[it]
        for w in range(4):
            s = sims[2 * w + it]
            up = from_above(s)
            dn = from_below(s)
            for b in range(BPI):
                e = pltpu.roll(ge, (96 - 6 * (4 * b + w)) % LANES, 1)
                parts = (
                    pltpu.roll(up, (LANES - WIN * b) % LANES, 1) if b else up,
                    pltpu.roll(s, (LANES + WIN - WIN * b) % LANES, 1) if b != 1 else s,
                    pltpu.roll(dn, (LANES + 2 * WIN - WIN * b) % LANES, 1) if b != 2 else dn,
                    jnp.where(lane < 102, e, 1.0),
                )
                x = quarters(lane, parts).astype(BF)
                at = group * w + ROWS * b
                xs[at : at + ROWS, 0:LANES] = x
                xs[at : at + ROWS, LANES : 2 * LANES] = x
        x = xs[...]
        for n in range(4):
            h = jnp.dot(x, w1_ref[:, 256 * n : 256 * (n + 1)], preferred_element_type=F)
            hs[:, 256 * n : 256 * (n + 1)] = jnp.maximum(h.astype(BF), jnp.zeros((), BF))

        @pl.when(it == 0)
        def _():
            hs[0:ROWS, 0:32] = jnp.zeros((ROWS, 32), BF)

        @pl.when(it == BLOCKS // BPI - 1)
        def _():
            hs[4 * group - ROWS : 4 * group, WIN * 32 - 32 : WIN * 32] = jnp.zeros((ROWS, 32), BF)

        p = [
            jnp.dot(
                hs[group * w : group * (w + 1), :], w2_ref[:, LANES * w : LANES * (w + 1)], preferred_element_type=F
            )
            for w in range(4)
        ]
        tot = jnp.zeros((ROWS, LANES), F)
        for b in range(BPI):
            k = it * BPI + b
            pb = [p[w][ROWS * b : ROWS * (b + 1)] for w in range(4)]
            a0 = quarters(lane, pb)
            a1 = pltpu.roll(quarters(lane, [pb[3], pb[0], pb[1], pb[2]]), LANES - WIN, 1)
            a2 = pltpu.roll(quarters(lane, [pb[2], pb[3], pb[0], pb[1]]), LANES - 2 * WIN, 1)
            acc[k] = a1 + from_above(a0) + from_below(a2)
            for w in range(4):
                at = 6 * (4 * b + w)
                moved = pltpu.roll(pb[w], (at + LANES - WIN * ((w + 3) % 4)) % LANES, 1)
                tot = jnp.where((lane >= at) & (lane < at + 6), moved, tot)
        ee[it] = tot
        return carry

    lax.fori_loop(0, BLOCKS // BPI, step, 0)
    kind = lax.rem(lane, 3)
    his, los = [], []
    for half in range(2):
        hi, lo = settle(kind, ee[half])
        his.append(hi)
        los.append(lo)
    hi = jnp.concatenate(his, axis=1)
    lo = jnp.concatenate(los, axis=1)
    for k in range(0, BLOCKS, 2):
        pick = sel2_ref[:, LANES * k : LANES * (k + 2)]
        extra = jnp.dot(hi, pick, preferred_element_type=F) + jnp.dot(lo, pick, preferred_element_type=F)
        for u in range(2):
            total = acc[k + u] + extra[:, LANES * u : LANES * (u + 1)]
            if k + u == 0:
                part_ref[0] = total
            elif k + u == BLOCKS - 1:
                part_ref[1] = total
            else:
                out_ref[:, LANES * (k + u) : LANES * (k + u + 1)] = total.astype(BF)


def settle(kind, v):
    c = jnp.where(kind == 0, from_above(v), jnp.where(kind == 1, v, from_below(v)))
    hi = c.astype(BF)
    return hi, (c - hi.astype(F)).astype(BF)


def sides_body(
    ends_ref, left_ref, right_ref, own_ref, part_ref, w1x_ref, w2x_ref, selx_ref, sel3_ref, old_ref,
    out_ref, held, sems,
):
    del old_ref
    lane = lax.broadcasted_iota(I, (ROWS, LANES), 1)
    near = jnp.concatenate([left_ref[...], right_ref[...]], axis=1)
    g0 = jnp.where(lane >= 96, own_ref[...], 0.0) + jnp.dot(near, selx_ref[...], preferred_element_type=F)
    g = g0 + pltpu.roll(from_above(g0), LANES - 1, 1) + pltpu.roll(from_below(g0), 1, 1)
    xw = jnp.where((lane >= 120) & (lane < 123), 1.0, g).astype(BF)
    hx = jnp.dot(xw, w1x_ref[0:LANES, :], preferred_element_type=F)
    hx = hx + jnp.dot(xw, w1x_ref[LANES : 2 * LANES, :], preferred_element_type=F)
    live = jnp.where(lane < 32, ends_ref[0], jnp.where(lane >= 96, ends_ref[1], 1))
    hx = jnp.maximum(hx, 0.0) * live.astype(F)
    sums = jnp.dot(hx.astype(BF), w2x_ref[...], preferred_element_type=F)
    hi, lo = settle(lax.rem(lane, 3), sums)
    extra = jnp.dot(hi, sel3_ref[...], preferred_element_type=F) + jnp.dot(lo, sel3_ref[...], preferred_element_type=F)
    copies = []
    for side in range(2):
        held[side] = (part_ref[side] + extra[:, LANES * side : LANES * (side + 1)]).astype(BF)
        block = out_ref.at[:, pl.ds(side * (COLS - LANES), LANES)]
        copies.append(pltpu.make_async_copy(held.at[side], block, sems.at[side]))
        copies[-1].start()
    for copy in copies:
        copy.wait()


SIDE_LANE = {0: 97, 1: 100, COLS - 2: 103, COLS - 1: 106, -2: 109, -1: 112, COLS: 115, COLS + 1: 118}
SIDE_HIDDEN = (-1, 0, COLS - 1, COLS)


def selectors():
    i, l = np.indices((COLS, 2 * LANES))
    i = i % WIN + WIN * (i // (BLOCKS * WIN)) + LANES * (i // WIN % BLOCKS)
    m, s = 16 * (l // LANES) + (l % LANES) // 6, (l % LANES) % 6
    fit = l % LANES < 96
    hit = (fit & (s == 1) & (i == WIN * m - 1)) | (fit & (s == 4) & (i == WIN * m + WIN))
    for c in (0, 1, COLS - 2, COLS - 1):
        hit = hit | ((l == SIDE_LANE[c]) & (i == c))
    sel1 = hit.astype(BF)
    i, l = np.indices((2 * LANES, LANES))
    hit = np.zeros((2 * LANES, LANES), bool)
    for row, c in ((LANES - 2, -2), (LANES - 1, -1), (LANES, COLS), (LANES + 1, COLS + 1)):
        hit = hit | ((i == row) & (l == SIDE_LANE[c]))
    selx = hit.astype(BF)
    l, j = np.indices((2 * LANES, COLS))
    m, s = 16 * (l // LANES) + (l % LANES) // 6, (l % LANES) % 6
    fit = l % LANES < 96
    sel2 = ((fit & (s < 3) & (j == WIN * m - 1)) | (fit & (s >= 3) & (j == WIN * m + WIN))).astype(BF)
    l, j = np.indices((LANES, 2 * LANES))
    hit = np.zeros((LANES, 2 * LANES), bool)
    for n, c in enumerate((0, 1, 2 * LANES - 2, 2 * LANES - 1)):
        hit = hit | ((l // 3 == n) & (j == c))
    return sel1, sel2, selx, hit.astype(BF)


def patterns():
    width = WIN * 32
    rows1, hit1, rowsx, hitx, lanes2, hit2, lanesy, hity = ([] for _ in range(8))
    for b in range(3):
        k, n = np.indices((LANES, width))
        pos, inner = n // 32, k % WIN
        hit1.append(
            ((k < 96) & (inner == pos + b - 1))
            | ((b == 0) & (k >= 96) & (k < 99) & (pos == 0))
            | ((b == 2) & (k >= 99) & (k < 102) & (pos == WIN - 1))
            | ((b == 1) & (k >= 102) & (k < 105))
        )
        k, tap = np.indices((LANES, 16))
        rows1.append(
            ((k < 96) & (tap == 3 * (k // WIN) + b))
            | ((b == 0) & (k >= 96) & (k < 99) & (tap == 3 * (k - 96)))
            | ((b == 2) & (k >= 99) & (k < 102) & (tap == 3 * (k - 99) + 2))
            | ((b == 1) & (k >= 102) & (k < 105) & (tap == k - 102 + 9))
        )
        k, n = np.indices((LANES, LANES))
        hit = (b == 1) & (k >= 120) & (k < 123)
        for h, c in enumerate(SIDE_HIDDEN):
            first = SIDE_LANE[c + b - 1] - 1
            hit = hit | ((n // 32 == h) & (k >= first) & (k < first + 3))
        hitx.append(hit)
        k, tap = np.indices((LANES, 16))
        row = (b == 1) & (k >= 120) & (k < 123) & (tap == k - 120 + 9)
        for middle in SIDE_LANE.values():
            row = row | ((k >= middle - 1) & (k <= middle + 1) & (tap == 3 * (k - middle + 1) + b))
        rowsx.append(row)
        n, l = np.indices((width, LANES))
        pos, inner = n // 32, l % WIN
        hit2.append(
            ((l < 96) & (inner == pos + 1 - b))
            | ((b == 2) & (l >= 96) & (l < 99) & (pos == 0))
            | ((b == 0) & (l >= 99) & (l < 102) & (pos == WIN - 1))
        )
        tap, l = np.indices((16, LANES))
        lanes2.append(
            ((l < 96) & (tap == 3 * (l // WIN) + b))
            | ((b == 2) & (l >= 96) & (l < 99) & (tap == 3 * (l - 96) + 2))
            | ((b == 0) & (l >= 99) & (l < 102) & (tap == 3 * (l - 99)))
        )
        n, l = np.indices((LANES, LANES))
        hit = np.zeros((LANES, LANES), bool)
        for h, c in enumerate(SIDE_HIDDEN):
            for j, out in enumerate((0, 1, COLS - 2, COLS - 1)):
                if c == out + b - 1:
                    hit = hit | ((n // 32 == h) & (l // 3 == j))
        hity.append(hit)
        tap, l = np.indices((16, LANES))
        lanesy.append((l < 12) & (tap == 3 * (l % 3) + b))
    i, n = np.indices((32, width))
    spread = i == n % 32
    groups = (rows1, hit1, rowsx, hitx, lanes2, hit2, lanesy, hity)
    return (spread.astype(BF), spread.T.astype(BF)) + tuple(np.stack(g).astype(BF) for g in groups)


def tables_body(
    first_ref, second_ref, spread_ref, tall_ref, rows1, hit1, rowsx, hitx, lanes2, hit2, lanesy, hity,
    w1_ref, w2_ref, w1x_ref, w2x_ref,
):
    dot = functools.partial(jnp.dot, preferred_element_type=F)
    raw = first_ref[...]
    hi = raw.astype(BF).astype(F)
    mid = (raw - hi).astype(BF).astype(F)
    low = raw - hi - mid
    row = lax.broadcasted_iota(I, raw.shape, 0)
    parts = (
        jnp.where(row == 10, mid, jnp.where(row == 11, low, hi)),
        jnp.where(row < 9, mid, 0.0),
    )
    for n, part in enumerate(parts):
        wide = dot(part.astype(BF), spread_ref[...]).astype(BF)
        at = slice(LANES * n, LANES * (n + 1))
        w1_ref[at, :] = sum(hit1[b].astype(F) * dot(rows1[b], wide) for b in range(3)).astype(BF)
        w1x_ref[at, :] = sum(hitx[b].astype(F) * dot(rowsx[b], wide[:, :LANES]) for b in range(3)).astype(BF)
    second = second_ref[...]
    tall = tall_ref[...]
    base = sum(
        hit2[b].astype(F) * dot(tall, dot(second, lanes2[b]).astype(BF)) for b in range(3)
    )
    for w in range(4):
        turned = pltpu.roll(base, WIN * w, 1) if w else base
        w2_ref[:, LANES * w : LANES * (w + 1)] = turned.astype(BF)
    w2x_ref[...] = sum(
        hity[b].astype(F) * dot(tall[:LANES], dot(second, lanesy[b]).astype(BF)) for b in range(3)
    ).astype(BF)


def weights(w_first, b_first, w_second):
    first = jnp.concatenate([w_first, jnp.broadcast_to(b_first[None], (3, 32)), jnp.zeros((4, 32), F)])
    second = jnp.pad(w_second.T, ((0, 0), (0, 7)))
    consts = patterns()
    vmem = pl.BlockSpec(memory_space=pltpu.VMEM)
    shapes = ((2 * LANES, WIN * 32), (WIN * 32, 4 * LANES), (2 * LANES, LANES), (LANES, LANES))
    return pl.pallas_call(
        tables_body,
        out_shape=tuple(jax.ShapeDtypeStruct(shape, BF) for shape in shapes),
        in_specs=[vmem] * (2 + len(consts)),
        out_specs=(vmem,) * 4,
        compiler_params=pltpu.CompilerParams(vmem_limit_bytes=24 * 1024 * 1024),
        cost_estimate=pl.CostEstimate(flops=0, bytes_accessed=60_000_000, transcendentals=0),
        name="tables",
    )(first, second, *consts)


def refine(mask, scores, tables):
    vmem = pl.BlockSpec(memory_space=pltpu.VMEM)
    hbm = pl.BlockSpec(memory_space=pltpu.HBM)
    arrays = tables
    return pl.pallas_call(
        refine_body,
        out_shape=(
            jax.ShapeDtypeStruct((ROWS, COLS), BF),
            jax.ShapeDtypeStruct((ROWS, LANES), F),
            jax.ShapeDtypeStruct((2, ROWS, LANES), F),
        ),
        in_specs=[pl.BlockSpec(memory_space=pltpu.SMEM), vmem] + [hbm] * len(arrays),
        out_specs=(vmem, vmem, vmem),
        scratch_shapes=[
            pltpu.VMEM((BLOCKS, ROWS, LANES), F),
            pltpu.VMEM((2, ROWS, LANES), F),
            pltpu.VMEM((4 * ROWS * BPI, 2 * LANES), BF),
            pltpu.VMEM((4 * ROWS * BPI, WIN * 32), BF),
            pltpu.VMEM((BLOCKS, ROWS, LANES), F),
            pltpu.VMEM((2, ROWS, LANES), F),
        ]
        + [pltpu.VMEM(array.shape, BF) for array in arrays]
        + [pltpu.SemaphoreType.DMA((len(arrays),))],
        compiler_params=pltpu.CompilerParams(vmem_limit_bytes=36 * 1024 * 1024),
        cost_estimate=pl.CostEstimate(flops=9_400_000_000, bytes_accessed=8_000_000, transcendentals=0),
        name="refine",
    )(mask, scores, *arrays)


def sides(ends, left, right, own, part, tables, out):
    vmem = pl.BlockSpec(memory_space=pltpu.VMEM)
    any_space = pl.BlockSpec(memory_space=pl.ANY)
    return pl.pallas_call(
        sides_body,
        out_shape=jax.ShapeDtypeStruct((ROWS, COLS), BF),
        in_specs=[pl.BlockSpec(memory_space=pltpu.SMEM)] + [vmem] * 8 + [any_space],
        out_specs=any_space,
        scratch_shapes=[pltpu.VMEM((2, ROWS, LANES), BF), pltpu.SemaphoreType.DMA((2,))],
        input_output_aliases={9: 0},
        compiler_params=pltpu.CompilerParams(vmem_limit_bytes=8 * 1024 * 1024),
        cost_estimate=pl.CostEstimate(flops=60_000_000, bytes_accessed=1_500_000, transcendentals=0),
        name="sides",
    )(ends, left, right, own, part, *tables, out)


def score_body(seat_ref, slab_ref, *rest):
    q_refs, out_ref = rest[:-1], rest[-1]
    side = len(q_refs)
    slab = slab_ref[...].swapaxes(0, 1).reshape(BLOCKS * WIN, slab_ref.shape[3])
    for step, q_ref in enumerate(q_refs):
        v = lax.rem(seat_ref[0] + side - step, side)
        out_ref[v] = lax.dot_general(q_ref[...], slab, NT, preferred_element_type=F).astype(BF)


def score(seat, slab, videos):
    vmem = pl.BlockSpec(memory_space=pltpu.VMEM)
    return pl.pallas_call(
        score_body,
        out_shape=jax.ShapeDtypeStruct((len(videos), ROWS, BLOCKS * WIN), BF),
        in_specs=[pl.BlockSpec(memory_space=pltpu.SMEM), vmem] + [vmem] * len(videos),
        out_specs=vmem,
        compiler_params=pltpu.CompilerParams(vmem_limit_bytes=12 * 1024 * 1024),
        cost_estimate=pl.CostEstimate(flops=540_000_000, bytes_accessed=3_100_000, transcendentals=0),
        name="score",
    )(seat, slab, *videos)


def pack_body(me_ref, time_ref, panels_ref, out_ref, zero_ref, sems):
    me = me_ref[0]
    first = me - lax.rem(me, 2)
    jobs = []
    for i in range(2 * BLOCKS):
        owner = time_ref[first * BLOCKS + i] // BLOCKS
        chip = owner // 2
        chip = jnp.where(lax.rem(me, 2) == 0, chip, out_ref.shape[0] // 2 - 1 - chip)
        slot = 2 * chip + i // BLOCKS
        copy = pltpu.make_async_copy(panels_ref.at[i], out_ref.at[slot], sems.at[i])
        jobs.append((lax.rem(owner, 2) == lax.rem(me, 2), copy))
    for wanted, copy in jobs:
        pl.when(wanted)(copy.start)
    zero_ref[...] = jnp.zeros(zero_ref.shape, F)
    for wanted, copy in jobs:
        pl.when(wanted)(copy.wait)


def pack(me, panel_time, panels, owners):
    any_space = pl.BlockSpec(memory_space=pl.ANY)
    smem = pl.BlockSpec(memory_space=pltpu.SMEM)
    return pl.pallas_call(
        pack_body,
        out_shape=(
            jax.ShapeDtypeStruct((owners,) + panels.shape[1:], BF),
            jax.ShapeDtypeStruct((8, LANES), F),
        ),
        in_specs=[smem, smem, any_space],
        out_specs=(any_space, pl.BlockSpec(memory_space=pltpu.VMEM)),
        scratch_shapes=[pltpu.SemaphoreType.DMA((2 * BLOCKS,))],
        compiler_params=pltpu.CompilerParams(vmem_limit_bytes=4 * 1024 * 1024),
        cost_estimate=pl.CostEstimate(flops=0, bytes_accessed=600_000, transcendentals=0),
        name="pack",
    )(me, panel_time, panels)


def share_body(q_ref, *rest):
    out_ref = rest[-1]
    out_ref[...] = q_ref[...]


def share(queries, after):
    vmem = pl.BlockSpec(memory_space=pltpu.VMEM)
    return pl.pallas_call(
        share_body,
        out_shape=jax.ShapeDtypeStruct(queries.shape, BF),
        in_specs=[vmem] + [pl.BlockSpec(memory_space=pl.ANY)] * len(after),
        out_specs=vmem,
        compiler_params=pltpu.CompilerParams(vmem_limit_bytes=4 * 1024 * 1024),
        cost_estimate=pl.CostEstimate(flops=0, bytes_accessed=1_000_000, transcendentals=0),
        name="share",
    )(queries, *after)


def place_body(source_ref, incoming_ref, *rest):
    out_ref, held, in_sems, out_sems = rest[-4:]
    gets = [
        pltpu.make_async_copy(incoming_ref.at[source_ref[k]], held.at[k], in_sems.at[k]) for k in range(BLOCKS)
    ]
    for copy in gets:
        copy.start()
    for copy in gets:
        copy.wait()
    puts = [pltpu.make_async_copy(held, out_ref.at[d], out_sems.at[d]) for d in range(out_ref.shape[0])]
    for copy in puts:
        copy.start()
    for copy in puts:
        copy.wait()


def place(source, incoming, copies, ready):
    any_space = pl.BlockSpec(memory_space=pl.ANY)
    piece = incoming.shape[1:]
    return pl.pallas_call(
        place_body,
        out_shape=jax.ShapeDtypeStruct((copies, BLOCKS) + piece, BF),
        in_specs=[pl.BlockSpec(memory_space=pltpu.SMEM)] + [any_space] * (1 + len(ready)),
        out_specs=any_space,
        scratch_shapes=[
            pltpu.VMEM((BLOCKS,) + piece, BF),
            pltpu.SemaphoreType.DMA((BLOCKS,)),
            pltpu.SemaphoreType.DMA((copies,)),
        ],
        compiler_params=pltpu.CompilerParams(vmem_limit_bytes=4 * 1024 * 1024),
        cost_estimate=pl.CostEstimate(flops=0, bytes_accessed=400_000_000, transcendentals=0),
        name="place",
    )(source, incoming, *ready)


def shards(queries, ref_panels, cand_mask, panel_time, w_first, b_first, w_second):
    owners = lax.axis_size("ref")
    fan = lax.axis_size("qry")
    me = lax.axis_index("ref")
    up = [(i, i + 1) for i in range(owners - 1)]
    down = [(i + 1, i) for i in range(owners - 1)]
    pairs = [[2 * z, 2 * z + 1] for z in range(owners // 2)]
    lines = [[2 * z + c for z in range(owners // 2)][:: 1 - 2 * c] for c in range(2)]
    side = LANES // WIN
    outer = [[i + side * j for j in range(side)] for i in range(fan // side)]
    inner = [[side * j + i for i in range(side)] for j in range(fan // side)]
    chip = lax.all_gather(ref_panels, "ref", axis=0, tiled=True, axis_index_groups=pairs)
    packed, zero = pack(me[None], panel_time, chip, owners)
    incoming = lax.all_to_all(packed, "ref", 0, 0, tiled=True, axis_index_groups=lines)
    holder = jnp.arange(owners * BLOCKS, dtype=I) // BLOCKS
    mine = panel_time[None, :] == me * BLOCKS + jnp.arange(BLOCKS, dtype=I)[:, None]
    source = jnp.sum(jnp.where(mine, holder[None, :], 0), axis=1)
    source = jnp.where(me % 2 == 0, source, owners - 2 - source + 2 * (source % 2))
    ends = jnp.stack([(me > 0).astype(I), (me < owners - 1).astype(I)])
    w1, w2, w1x, w2x = weights(w_first, b_first, w_second)
    sel1, sel2, selx, sel3 = selectors()

    shared = share(queries, (zero, w1, w2, w1x, w2x))
    videos = [shared] + [
        lax.ppermute(
            shared, "qry", [(g[i], g[(i + step) % side]) for g in outer for i in range(side)]
        )
        for step in range(1, side)
    ]
    seat = lax.axis_index("qry") // (fan // side)

    rows = [jnp.repeat(cand_mask[:, c].astype(BF), ROWS // 2)[:, None] for c in (0, BLOCKS - 1)]
    ready = (w1, w2, w1x, w2x, ends) + tuple(rows)
    slab = lax.all_to_all(
        place(source, incoming, side, ready), "qry", 0, 0, tiled=True, axis_index_groups=inner
    )
    scores = lax.all_to_all(score(seat[None], slab, videos), "qry", 0, 0, tiled=True, axis_index_groups=outer)
    head = scores[0, :, :LANES] * rows[0]
    tail = scores[side - 1, :, LANES:] * rows[1]
    from_left = lax.ppermute(tail, "ref", up)
    from_right = lax.ppermute(head, "ref", down)
    out, own, part = refine(cand_mask, scores, (sel1, w1, w2, sel2))
    return sides(ends, from_left, from_right, own, part, (w1x, w2x, selx, sel3), out)


def solution(mesh):
    placed = (P("qry", None), P("ref", "qry", None), P("qry", "ref"), P(), P(), P(), P())
    return jax.shard_map(
        shards, mesh=mesh, in_specs=placed, out_specs=P("qry", "ref"), check_vma=False
    )
```

```python
import functools

import jax
import jax.numpy as jnp
import numpy as np
from jax import lax
from jax.experimental import pallas as pl
from jax.experimental.pallas import tpu as pltpu
from jax.sharding import PartitionSpec as P

BF = jnp.bfloat16
F = jnp.float32
I = jnp.int32
NT = (((1,), (1,)), ((), ()))
ROWS = 256
COLS = 1024
BLOCKS = 8
LANES = 128
WIN = 32
BPI = 4


def from_above(v):
    row = lax.broadcasted_iota(I, v.shape, 0)
    return jnp.where(row == 0, 0.0, pltpu.roll(v, 1, 0))


def from_below(v):
    row = lax.broadcasted_iota(I, v.shape, 0)
    n = v.shape[0]
    return jnp.where(row == n - 1, 0.0, pltpu.roll(v, n - 1, 0))


def quarters(lane, four):
    return jnp.where(
        lane < 64,
        jnp.where(lane < 32, four[0], four[1]),
        jnp.where(lane < 96, four[2], four[3]),
    )


def refine_body(
    mask_ref, score_ref, sel1_ref, w1_ref, w2_ref, sel2_ref,
    out_ref, own_ref, part_ref, sims, gg, xs, hs, acc, ee,
):
    lane = lax.broadcasted_iota(I, (ROWS, LANES), 1)
    top = lax.broadcasted_iota(I, (ROWS, LANES), 0) < ROWS // 2
    keep = []
    for half in range(2):
        rows = [quarters(lane, [mask_ref[r, 4 * half + j] for j in range(4)]) for r in range(2)]
        keep.append(jnp.where(top, rows[0], rows[1]).astype(F))
    g0 = jnp.zeros((ROWS, 2 * LANES), F)
    for n in range(BLOCKS):
        half = n % 2
        v = score_ref[n // 2, :, LANES * half : LANES * (half + 1)].astype(F) * keep[half]
        sims[n] = v
        g0 = g0 + jnp.dot(v.astype(BF), sel1_ref[LANES * n : LANES * (n + 1), :], preferred_element_type=F)
    own_ref[...] = g0[:, :LANES]
    g = g0 + pltpu.roll(from_above(g0), 2 * LANES - 1, 1) + pltpu.roll(from_below(g0), 1, 1)
    gg[0] = g[:, :LANES]
    gg[1] = g[:, LANES:]
    group = ROWS * BPI

    zero = jnp.zeros((), BF)

    def step(it, carry):
        ge = gg[it].astype(BF)
        one = jnp.ones((), BF)
        p = []
        for w in range(4):
            s = sims[2 * w + it]
            up = from_above(s).astype(BF)
            dn = from_below(s).astype(BF)
            s = s.astype(BF)
            for b in range(BPI):
                e = pltpu.roll(ge, (96 - 6 * (4 * b + w)) % LANES, 1)
                parts = (
                    pltpu.roll(up, (LANES - WIN * b) % LANES, 1) if b else up,
                    pltpu.roll(s, (LANES + WIN - WIN * b) % LANES, 1) if b != 1 else s,
                    pltpu.roll(dn, (LANES + 2 * WIN - WIN * b) % LANES, 1) if b != 2 else dn,
                    jnp.where(lane < 102, e, one),
                )
                x = quarters(lane, parts)
                at = group * w + ROWS * b
                xs[at : at + ROWS, 0:LANES] = x
                xs[at : at + ROWS, LANES : 2 * LANES] = x
            at = slice(group * w, group * (w + 1))
            x = xs[at, :]
            for n in range(2):
                h = jnp.dot(x, w1_ref[:, 512 * n : 512 * (n + 1)], preferred_element_type=F)
                hs[at, 512 * n : 512 * (n + 1)] = jnp.maximum(h.astype(BF), zero)
            if w == 0:
                hs[0:ROWS, 0:32] = jnp.where(it == 0, zero, hs[0:ROWS, 0:32])
            if w == 3:
                end = slice(4 * group - ROWS, 4 * group), slice(WIN * 32 - 32, WIN * 32)
                hs[end] = jnp.where(it == BLOCKS // BPI - 1, zero, hs[end])
            p.append(jnp.dot(hs[at, :], w2_ref[:, LANES * w : LANES * (w + 1)], preferred_element_type=F))
        tot = jnp.zeros((ROWS, LANES), F)
        for b in range(BPI):
            k = it * BPI + b
            pb = [p[w][ROWS * b : ROWS * (b + 1)] for w in range(4)]
            a0 = quarters(lane, pb)
            a1 = pltpu.roll(quarters(lane, [pb[3], pb[0], pb[1], pb[2]]), LANES - WIN, 1)
            a2 = pltpu.roll(quarters(lane, [pb[2], pb[3], pb[0], pb[1]]), LANES - 2 * WIN, 1)
            acc[k] = a1 + from_above(a0) + from_below(a2)
            for w in range(4):
                at = 6 * (4 * b + w)
                moved = pltpu.roll(pb[w], (at + LANES - WIN * ((w + 3) % 4)) % LANES, 1)
                tot = jnp.where((lane >= at) & (lane < at + 6), moved, tot)
        ee[it] = tot
        return carry

    lax.fori_loop(0, BLOCKS // BPI, step, 0)
    kind = lax.rem(lane, 3)
    his, los = [], []
    for half in range(2):
        hi, lo = settle(kind, ee[half])
        his.append(hi)
        los.append(lo)
    hi = jnp.concatenate(his, axis=1)
    lo = jnp.concatenate(los, axis=1)
    for k in range(0, BLOCKS, 2):
        pick = sel2_ref[:, LANES * k : LANES * (k + 2)]
        extra = jnp.dot(hi, pick, preferred_element_type=F) + jnp.dot(lo, pick, preferred_element_type=F)
        for u in range(2):
            total = acc[k + u] + extra[:, LANES * u : LANES * (u + 1)]
            if k + u == 0:
                part_ref[0] = total
            elif k + u == BLOCKS - 1:
                part_ref[1] = total
            else:
                out_ref[:, LANES * (k + u) : LANES * (k + u + 1)] = total.astype(BF)


def settle(kind, v):
    c = jnp.where(kind == 0, from_above(v), jnp.where(kind == 1, v, from_below(v)))
    hi = c.astype(BF)
    return hi, (c - hi.astype(F)).astype(BF)


def sides_body(
    ends_ref, left_ref, right_ref, own_ref, part_ref, w1x_ref, w2x_ref, selx_ref, sel3_ref, old_ref,
    out_ref, held, sems,
):
    del old_ref
    lane = lax.broadcasted_iota(I, (ROWS, LANES), 1)
    near = jnp.concatenate([left_ref[...], right_ref[...]], axis=1)
    g0 = jnp.where(lane >= 96, own_ref[...], 0.0) + jnp.dot(near, selx_ref[...], preferred_element_type=F)
    g = g0 + pltpu.roll(from_above(g0), LANES - 1, 1) + pltpu.roll(from_below(g0), 1, 1)
    xw = jnp.where((lane >= 120) & (lane < 123), 1.0, g).astype(BF)
    hx = jnp.dot(xw, w1x_ref[0:LANES, :], preferred_element_type=F)
    hx = hx + jnp.dot(xw, w1x_ref[LANES : 2 * LANES, :], preferred_element_type=F)
    live = jnp.where(lane < 32, ends_ref[0], jnp.where(lane >= 96, ends_ref[1], 1))
    hx = jnp.maximum(hx, 0.0) * live.astype(F)
    sums = jnp.dot(hx.astype(BF), w2x_ref[...], preferred_element_type=F)
    hi, lo = settle(lax.rem(lane, 3), sums)
    extra = jnp.dot(hi, sel3_ref[...], preferred_element_type=F) + jnp.dot(lo, sel3_ref[...], preferred_element_type=F)
    copies = []
    for side in range(2):
        held[side] = (part_ref[side] + extra[:, LANES * side : LANES * (side + 1)]).astype(BF)
        block = out_ref.at[:, pl.ds(side * (COLS - LANES), LANES)]
        copies.append(pltpu.make_async_copy(held.at[side], block, sems.at[side]))
        copies[-1].start()
    for copy in copies:
        copy.wait()


SIDE_LANE = {0: 97, 1: 100, COLS - 2: 103, COLS - 1: 106, -2: 109, -1: 112, COLS: 115, COLS + 1: 118}
SIDE_HIDDEN = (-1, 0, COLS - 1, COLS)


def selectors():
    i, l = np.indices((COLS, 2 * LANES))
    i = i % WIN + WIN * (i // (BLOCKS * WIN)) + LANES * (i // WIN % BLOCKS)
    m, s = 16 * (l // LANES) + (l % LANES) // 6, (l % LANES) % 6
    fit = l % LANES < 96
    hit = (fit & (s == 1) & (i == WIN * m - 1)) | (fit & (s == 4) & (i == WIN * m + WIN))
    for c in (0, 1, COLS - 2, COLS - 1):
        hit = hit | ((l == SIDE_LANE[c]) & (i == c))
    sel1 = hit.astype(BF)
    i, l = np.indices((2 * LANES, LANES))
    hit = np.zeros((2 * LANES, LANES), bool)
    for row, c in ((LANES - 2, -2), (LANES - 1, -1), (LANES, COLS), (LANES + 1, COLS + 1)):
        hit = hit | ((i == row) & (l == SIDE_LANE[c]))
    selx = hit.astype(BF)
    l, j = np.indices((2 * LANES, COLS))
    m, s = 16 * (l // LANES) + (l % LANES) // 6, (l % LANES) % 6
    fit = l % LANES < 96
    sel2 = ((fit & (s < 3) & (j == WIN * m - 1)) | (fit & (s >= 3) & (j == WIN * m + WIN))).astype(BF)
    l, j = np.indices((LANES, 2 * LANES))
    hit = np.zeros((LANES, 2 * LANES), bool)
    for n, c in enumerate((0, 1, 2 * LANES - 2, 2 * LANES - 1)):
        hit = hit | ((l // 3 == n) & (j == c))
    return sel1, sel2, selx, hit.astype(BF)


def patterns():
    width = WIN * 32
    rows1, hit1, rowsx, hitx, lanes2, hit2, lanesy, hity = ([] for _ in range(8))
    for b in range(3):
        k, n = np.indices((LANES, width))
        pos, inner = n // 32, k % WIN
        hit1.append(
            ((k < 96) & (inner == pos + b - 1))
            | ((b == 0) & (k >= 96) & (k < 99) & (pos == 0))
            | ((b == 2) & (k >= 99) & (k < 102) & (pos == WIN - 1))
            | ((b == 1) & (k >= 102) & (k < 105))
        )
        k, tap = np.indices((LANES, 16))
        rows1.append(
            ((k < 96) & (tap == 3 * (k // WIN) + b))
            | ((b == 0) & (k >= 96) & (k < 99) & (tap == 3 * (k - 96)))
            | ((b == 2) & (k >= 99) & (k < 102) & (tap == 3 * (k - 99) + 2))
            | ((b == 1) & (k >= 102) & (k < 105) & (tap == k - 102 + 9))
        )
        k, n = np.indices((LANES, LANES))
        hit = (b == 1) & (k >= 120) & (k < 123)
        for h, c in enumerate(SIDE_HIDDEN):
            first = SIDE_LANE[c + b - 1] - 1
            hit = hit | ((n // 32 == h) & (k >= first) & (k < first + 3))
        hitx.append(hit)
        k, tap = np.indices((LANES, 16))
        row = (b == 1) & (k >= 120) & (k < 123) & (tap == k - 120 + 9)
        for middle in SIDE_LANE.values():
            row = row | ((k >= middle - 1) & (k <= middle + 1) & (tap == 3 * (k - middle + 1) + b))
        rowsx.append(row)
        n, l = np.indices((width, LANES))
        pos, inner = n // 32, l % WIN
        hit2.append(
            ((l < 96) & (inner == pos + 1 - b))
            | ((b == 2) & (l >= 96) & (l < 99) & (pos == 0))
            | ((b == 0) & (l >= 99) & (l < 102) & (pos == WIN - 1))
        )
        tap, l = np.indices((16, LANES))
        lanes2.append(
            ((l < 96) & (tap == 3 * (l // WIN) + b))
            | ((b == 2) & (l >= 96) & (l < 99) & (tap == 3 * (l - 96) + 2))
            | ((b == 0) & (l >= 99) & (l < 102) & (tap == 3 * (l - 99)))
        )
        n, l = np.indices((LANES, LANES))
        hit = np.zeros((LANES, LANES), bool)
        for h, c in enumerate(SIDE_HIDDEN):
            for j, out in enumerate((0, 1, COLS - 2, COLS - 1)):
                if c == out + b - 1:
                    hit = hit | ((n // 32 == h) & (l // 3 == j))
        hity.append(hit)
        tap, l = np.indices((16, LANES))
        lanesy.append((l < 12) & (tap == 3 * (l % 3) + b))
    i, n = np.indices((32, width))
    spread = i == n % 32
    groups = (rows1, hit1, rowsx, hitx, lanes2, hit2, lanesy, hity)
    return (spread.astype(BF), spread.T.astype(BF)) + tuple(np.stack(g).astype(BF) for g in groups)


def tables_body(
    first_ref, second_ref, spread_ref, tall_ref, rows1, hit1, rowsx, hitx, lanes2, hit2, lanesy, hity,
    w1_ref, w2_ref, w1x_ref, w2x_ref,
):
    dot = functools.partial(jnp.dot, preferred_element_type=F)
    raw = first_ref[...]
    hi = raw.astype(BF).astype(F)
    mid = (raw - hi).astype(BF).astype(F)
    low = raw - hi - mid
    row = lax.broadcasted_iota(I, raw.shape, 0)
    parts = (
        jnp.where(row == 10, mid, jnp.where(row == 11, low, hi)),
        jnp.where(row < 9, mid, 0.0),
    )
    for n, part in enumerate(parts):
        wide = dot(part.astype(BF), spread_ref[...]).astype(BF)
        at = slice(LANES * n, LANES * (n + 1))
        w1_ref[at, :] = sum(hit1[b].astype(F) * dot(rows1[b], wide) for b in range(3)).astype(BF)
        w1x_ref[at, :] = sum(hitx[b].astype(F) * dot(rowsx[b], wide[:, :LANES]) for b in range(3)).astype(BF)
    second = second_ref[...]
    tall = tall_ref[...]
    base = sum(
        hit2[b].astype(F) * dot(tall, dot(second, lanes2[b]).astype(BF)) for b in range(3)
    )
    for w in range(4):
        turned = pltpu.roll(base, WIN * w, 1) if w else base
        w2_ref[:, LANES * w : LANES * (w + 1)] = turned.astype(BF)
    w2x_ref[...] = sum(
        hity[b].astype(F) * dot(tall[:LANES], dot(second, lanesy[b]).astype(BF)) for b in range(3)
    ).astype(BF)


def weights(w_first, b_first, w_second):
    first = jnp.concatenate([w_first, jnp.broadcast_to(b_first[None], (3, 32)), jnp.zeros((4, 32), F)])
    second = jnp.pad(w_second.T, ((0, 0), (0, 7)))
    consts = patterns()
    vmem = pl.BlockSpec(memory_space=pltpu.VMEM)
    shapes = ((2 * LANES, WIN * 32), (WIN * 32, 4 * LANES), (2 * LANES, LANES), (LANES, LANES))
    return pl.pallas_call(
        tables_body,
        out_shape=tuple(jax.ShapeDtypeStruct(shape, BF) for shape in shapes),
        in_specs=[vmem] * (2 + len(consts)),
        out_specs=(vmem,) * 4,
        compiler_params=pltpu.CompilerParams(vmem_limit_bytes=24 * 1024 * 1024),
        cost_estimate=pl.CostEstimate(flops=0, bytes_accessed=60_000_000, transcendentals=0),
        name="tables",
    )(first, second, *consts)


def refine(mask, scores, tables):
    vmem = pl.BlockSpec(memory_space=pltpu.VMEM)
    return pl.pallas_call(
        refine_body,
        out_shape=(
            jax.ShapeDtypeStruct((ROWS, COLS), BF),
            jax.ShapeDtypeStruct((ROWS, LANES), F),
            jax.ShapeDtypeStruct((2, ROWS, LANES), F),
        ),
        in_specs=[pl.BlockSpec(memory_space=pltpu.SMEM), vmem] + [vmem] * len(tables),
        out_specs=(vmem, vmem, vmem),
        scratch_shapes=[
            pltpu.VMEM((BLOCKS, ROWS, LANES), F),
            pltpu.VMEM((2, ROWS, LANES), F),
            pltpu.VMEM((4 * ROWS * BPI, 2 * LANES), BF),
            pltpu.VMEM((4 * ROWS * BPI, WIN * 32), BF),
            pltpu.VMEM((BLOCKS, ROWS, LANES), F),
            pltpu.VMEM((2, ROWS, LANES), F),
        ],
        compiler_params=pltpu.CompilerParams(vmem_limit_bytes=36 * 1024 * 1024),
        cost_estimate=pl.CostEstimate(flops=9_400_000_000, bytes_accessed=8_000_000, transcendentals=0),
        name="refine",
    )(mask, scores, *tables)


def sides(ends, left, right, own, part, tables, out):
    vmem = pl.BlockSpec(memory_space=pltpu.VMEM)
    any_space = pl.BlockSpec(memory_space=pl.ANY)
    return pl.pallas_call(
        sides_body,
        out_shape=jax.ShapeDtypeStruct((ROWS, COLS), BF),
        in_specs=[pl.BlockSpec(memory_space=pltpu.SMEM)] + [vmem] * 8 + [any_space],
        out_specs=any_space,
        scratch_shapes=[pltpu.VMEM((2, ROWS, LANES), BF), pltpu.SemaphoreType.DMA((2,))],
        input_output_aliases={9: 0},
        compiler_params=pltpu.CompilerParams(vmem_limit_bytes=8 * 1024 * 1024),
        cost_estimate=pl.CostEstimate(flops=60_000_000, bytes_accessed=1_500_000, transcendentals=0),
        name="sides",
    )(ends, left, right, own, part, *tables, out)


def score_body(seat_ref, slab_ref, *rest):
    q_refs, out_ref = rest[:-1], rest[-1]
    side = len(q_refs)
    slab = slab_ref[...].swapaxes(0, 1).reshape(BLOCKS * WIN, slab_ref.shape[3])
    for step, q_ref in enumerate(q_refs):
        v = lax.rem(seat_ref[0] + side - step, side)
        out_ref[v] = lax.dot_general(q_ref[...], slab, NT, preferred_element_type=F).astype(BF)


def score(seat, slab, videos):
    vmem = pl.BlockSpec(memory_space=pltpu.VMEM)
    return pl.pallas_call(
        score_body,
        out_shape=jax.ShapeDtypeStruct((len(videos), ROWS, BLOCKS * WIN), BF),
        in_specs=[pl.BlockSpec(memory_space=pltpu.SMEM), vmem] + [vmem] * len(videos),
        out_specs=vmem,
        compiler_params=pltpu.CompilerParams(vmem_limit_bytes=12 * 1024 * 1024),
        cost_estimate=pl.CostEstimate(flops=540_000_000, bytes_accessed=3_100_000, transcendentals=0),
        name="score",
    )(seat, slab, *videos)


def pack_body(me_ref, time_ref, panels_ref, out_ref, zero_ref, sems):
    me = me_ref[0]
    first = me - lax.rem(me, 2)
    jobs = []
    for i in range(2 * BLOCKS):
        owner = time_ref[first * BLOCKS + i] // BLOCKS
        chip = owner // 2
        chip = jnp.where(lax.rem(me, 2) == 0, chip, out_ref.shape[0] // 2 - 1 - chip)
        slot = 2 * chip + i // BLOCKS
        copy = pltpu.make_async_copy(panels_ref.at[i], out_ref.at[slot], sems.at[i])
        jobs.append((lax.rem(owner, 2) == lax.rem(me, 2), copy))
    for wanted, copy in jobs:
        pl.when(wanted)(copy.start)
    zero_ref[...] = jnp.zeros(zero_ref.shape, F)
    for wanted, copy in jobs:
        pl.when(wanted)(copy.wait)


def pack(me, panel_time, panels, owners):
    any_space = pl.BlockSpec(memory_space=pl.ANY)
    smem = pl.BlockSpec(memory_space=pltpu.SMEM)
    return pl.pallas_call(
        pack_body,
        out_shape=(
            jax.ShapeDtypeStruct((owners,) + panels.shape[1:], BF),
            jax.ShapeDtypeStruct((8, LANES), F),
        ),
        in_specs=[smem, smem, any_space],
        out_specs=(any_space, pl.BlockSpec(memory_space=pltpu.VMEM)),
        scratch_shapes=[pltpu.SemaphoreType.DMA((2 * BLOCKS,))],
        compiler_params=pltpu.CompilerParams(vmem_limit_bytes=4 * 1024 * 1024),
        cost_estimate=pl.CostEstimate(flops=0, bytes_accessed=600_000, transcendentals=0),
        name="pack",
    )(me, panel_time, panels)


def share_body(q_ref, *rest):
    out_ref = rest[-1]
    out_ref[...] = q_ref[...]


def share(queries, after):
    vmem = pl.BlockSpec(memory_space=pltpu.VMEM)
    return pl.pallas_call(
        share_body,
        out_shape=jax.ShapeDtypeStruct(queries.shape, BF),
        in_specs=[vmem] + [pl.BlockSpec(memory_space=pl.ANY)] * len(after),
        out_specs=vmem,
        compiler_params=pltpu.CompilerParams(vmem_limit_bytes=4 * 1024 * 1024),
        cost_estimate=pl.CostEstimate(flops=0, bytes_accessed=1_000_000, transcendentals=0),
        name="share",
    )(queries, *after)


def place_body(source_ref, incoming_ref, *rest):
    out_ref, sems = rest[-2:]
    copies = [
        pltpu.make_async_copy(incoming_ref.at[source_ref[k]], out_ref.at[d, k], sems.at[d, k])
        for k in range(BLOCKS)
        for d in range(out_ref.shape[0])
    ]
    for copy in copies:
        copy.start()
    for copy in copies:
        copy.wait()


def place(source, incoming, copies, ready):
    any_space = pl.BlockSpec(memory_space=pl.ANY)
    piece = incoming.shape[1:]
    return pl.pallas_call(
        place_body,
        out_shape=jax.ShapeDtypeStruct((copies, BLOCKS) + piece, BF),
        in_specs=[pl.BlockSpec(memory_space=pltpu.SMEM)] + [any_space] * (1 + len(ready)),
        out_specs=any_space,
        scratch_shapes=[pltpu.SemaphoreType.DMA((copies, BLOCKS))],
        compiler_params=pltpu.CompilerParams(vmem_limit_bytes=4 * 1024 * 1024),
        cost_estimate=pl.CostEstimate(flops=0, bytes_accessed=400_000_000, transcendentals=0),
        name="place",
    )(source, incoming, *ready)


def shards(queries, ref_panels, cand_mask, panel_time, w_first, b_first, w_second):
    owners = lax.axis_size("ref")
    fan = lax.axis_size("qry")
    me = lax.axis_index("ref")
    up = [(i, i + 1) for i in range(owners - 1)]
    down = [(i + 1, i) for i in range(owners - 1)]
    pairs = [[2 * z, 2 * z + 1] for z in range(owners // 2)]
    lines = [[2 * z + c for z in range(owners // 2)][:: 1 - 2 * c] for c in range(2)]
    side = LANES // WIN
    outer = [[i + side * j for j in range(side)] for i in range(fan // side)]
    inner = [[side * j + i for i in range(side)] for j in range(fan // side)]
    chip = lax.all_gather(ref_panels, "ref", axis=0, tiled=True, axis_index_groups=pairs)
    packed, zero = pack(me[None], panel_time, chip, owners)
    incoming = lax.all_to_all(packed, "ref", 0, 0, tiled=True, axis_index_groups=lines)
    holder = jnp.arange(owners * BLOCKS, dtype=I) // BLOCKS
    mine = panel_time[None, :] == me * BLOCKS + jnp.arange(BLOCKS, dtype=I)[:, None]
    source = jnp.sum(jnp.where(mine, holder[None, :], 0), axis=1)
    source = jnp.where(me % 2 == 0, source, owners - 2 - source + 2 * (source % 2))
    ends = jnp.stack([(me > 0).astype(I), (me < owners - 1).astype(I)])
    w1, w2, w1x, w2x = weights(w_first, b_first, w_second)
    sel1, sel2, selx, sel3 = selectors()

    shared = share(queries, (zero, w1, w2, w1x, w2x))
    videos = [shared] + [
        lax.ppermute(
            shared, "qry", [(g[i], g[(i + step) % side]) for g in outer for i in range(side)]
        )
        for step in range(1, side)
    ]
    seat = lax.axis_index("qry") // (fan // side)

    rows = [jnp.repeat(cand_mask[:, c].astype(BF), ROWS // 2)[:, None] for c in (0, BLOCKS - 1)]
    ready = (w1, w2, w1x, w2x, ends) + tuple(rows)
    slab = lax.all_to_all(
        place(source, incoming, side, ready), "qry", 0, 0, tiled=True, axis_index_groups=inner
    )
    scores = lax.all_to_all(score(seat[None], slab, videos), "qry", 0, 0, tiled=True, axis_index_groups=outer)
    head = scores[0, :, :LANES] * rows[0]
    tail = scores[side - 1, :, LANES:] * rows[1]
    from_left = lax.ppermute(tail, "ref", up)
    from_right = lax.ppermute(head, "ref", down)
    out, own, part = refine(cand_mask, scores, (sel1, w1, w2, sel2))
    return sides(ends, from_left, from_right, own, part, (w1x, w2x, selx, sel3), out)


def solution(mesh):
    placed = (P("qry", None), P("ref", "qry", None), P("qry", "ref"), P(), P(), P(), P())
    return jax.shard_map(
        shards, mesh=mesh, in_specs=placed, out_specs=P("qry", "ref"), check_vma=False
    )
```

```python
import functools

import jax
import jax.numpy as jnp
import numpy as np
from jax import lax
from jax.experimental import pallas as pl
from jax.experimental.pallas import tpu as pltpu
from jax.sharding import PartitionSpec as P

BF = jnp.bfloat16
F = jnp.float32
I = jnp.int32
NT = (((1,), (1,)), ((), ()))
ROWS = 256
COLS = 1024
BLOCKS = 8
LANES = 128
WIN = 32
BPI = 4


def from_above(v):
    row = lax.broadcasted_iota(I, v.shape, 0)
    return jnp.where(row == 0, 0.0, pltpu.roll(v, 1, 0))


def from_below(v):
    row = lax.broadcasted_iota(I, v.shape, 0)
    n = v.shape[0]
    return jnp.where(row == n - 1, 0.0, pltpu.roll(v, n - 1, 0))


def quarters(lane, four):
    return jnp.where(
        lane < 64,
        jnp.where(lane < 32, four[0], four[1]),
        jnp.where(lane < 96, four[2], four[3]),
    )


def refine_body(
    mask_ref, score_ref, sel1_ref, w1_ref, w2_ref, sel2_ref,
    out_ref, own_ref, part_ref, sims, gg, xs, hs, acc, ee,
):
    lane = lax.broadcasted_iota(I, (ROWS, LANES), 1)
    top = lax.broadcasted_iota(I, (ROWS, LANES), 0) < ROWS // 2
    keep = []
    for half in range(2):
        rows = [quarters(lane, [mask_ref[r, 4 * half + j] for j in range(4)]) for r in range(2)]
        keep.append(jnp.where(top, rows[0], rows[1]).astype(F))
    g0 = jnp.zeros((ROWS, 2 * LANES), F)
    for n in range(BLOCKS):
        half = n % 2
        v = score_ref[n // 2, :, LANES * half : LANES * (half + 1)].astype(F) * keep[half]
        sims[n] = v
        g0 = g0 + jnp.dot(v.astype(BF), sel1_ref[LANES * n : LANES * (n + 1), :], preferred_element_type=F)
    own_ref[...] = g0[:, :LANES]
    g = g0 + pltpu.roll(from_above(g0), 2 * LANES - 1, 1) + pltpu.roll(from_below(g0), 1, 1)
    gg[0] = g[:, :LANES]
    gg[1] = g[:, LANES:]
    group = ROWS * BPI

    zero = jnp.zeros((), BF)

    def step(it, carry):
        ge = gg[it].astype(BF)
        one = jnp.ones((), BF)
        p = []
        for w in range(4):
            s = sims[2 * w + it]
            up = from_above(s).astype(BF)
            dn = from_below(s).astype(BF)
            s = s.astype(BF)
            for b in range(BPI):
                e = pltpu.roll(ge, (96 - 6 * (4 * b + w)) % LANES, 1)
                parts = (
                    pltpu.roll(up, (LANES - WIN * b) % LANES, 1) if b else up,
                    pltpu.roll(s, (LANES + WIN - WIN * b) % LANES, 1) if b != 1 else s,
                    pltpu.roll(dn, (LANES + 2 * WIN - WIN * b) % LANES, 1) if b != 2 else dn,
                    jnp.where(lane < 102, e, one),
                )
                x = quarters(lane, parts)
                at = group * w + ROWS * b
                xs[at : at + ROWS, 0:LANES] = x
                xs[at : at + ROWS, LANES : 2 * LANES] = x
            at = slice(group * w, group * (w + 1))
            x = xs[at, :]
            for n in range(2):
                h = jnp.dot(x, w1_ref[:, 512 * n : 512 * (n + 1)], preferred_element_type=F)
                hs[at, 512 * n : 512 * (n + 1)] = jnp.maximum(h.astype(BF), zero)
            if w == 0:
                hs[0:ROWS, 0:32] = jnp.where(it == 0, zero, hs[0:ROWS, 0:32])
            if w == 3:
                end = slice(4 * group - ROWS, 4 * group), slice(WIN * 32 - 32, WIN * 32)
                hs[end] = jnp.where(it == BLOCKS // BPI - 1, zero, hs[end])
            p.append(jnp.dot(hs[at, :], w2_ref[:, LANES * w : LANES * (w + 1)], preferred_element_type=F))
        tot = jnp.zeros((ROWS, LANES), F)
        for b in range(BPI):
            k = it * BPI + b
            pb = [p[w][ROWS * b : ROWS * (b + 1)] for w in range(4)]
            a0 = quarters(lane, pb)
            a1 = pltpu.roll(quarters(lane, [pb[3], pb[0], pb[1], pb[2]]), LANES - WIN, 1)
            a2 = pltpu.roll(quarters(lane, [pb[2], pb[3], pb[0], pb[1]]), LANES - 2 * WIN, 1)
            acc[k] = a1 + from_above(a0) + from_below(a2)
            for w in range(4):
                at = 6 * (4 * b + w)
                moved = pltpu.roll(pb[w], (at + LANES - WIN * ((w + 3) % 4)) % LANES, 1)
                tot = jnp.where((lane >= at) & (lane < at + 6), moved, tot)
        ee[it] = tot
        return carry

    lax.fori_loop(0, BLOCKS // BPI, step, 0)
    kind = lax.rem(lane, 3)
    his, los = [], []
    for half in range(2):
        hi, lo = settle(kind, ee[half])
        his.append(hi)
        los.append(lo)
    hi = jnp.concatenate(his, axis=1)
    lo = jnp.concatenate(los, axis=1)
    for k in range(0, BLOCKS, 2):
        pick = sel2_ref[:, LANES * k : LANES * (k + 2)]
        extra = jnp.dot(hi, pick, preferred_element_type=F) + jnp.dot(lo, pick, preferred_element_type=F)
        for u in range(2):
            total = acc[k + u] + extra[:, LANES * u : LANES * (u + 1)]
            if k + u == 0:
                part_ref[0] = total
            elif k + u == BLOCKS - 1:
                part_ref[1] = total
            else:
                out_ref[:, LANES * (k + u) : LANES * (k + u + 1)] = total.astype(BF)


def settle(kind, v):
    c = jnp.where(kind == 0, from_above(v), jnp.where(kind == 1, v, from_below(v)))
    hi = c.astype(BF)
    return hi, (c - hi.astype(F)).astype(BF)


def sides_body(
    ends_ref, left_ref, right_ref, own_ref, part_ref, w1x_ref, w2x_ref, selx_ref, sel3_ref, old_ref,
    out_ref, held, sems,
):
    del old_ref
    lane = lax.broadcasted_iota(I, (ROWS, LANES), 1)
    near = jnp.concatenate([left_ref[...], right_ref[...]], axis=1)
    g0 = jnp.where(lane >= 96, own_ref[...], 0.0) + jnp.dot(near, selx_ref[...], preferred_element_type=F)
    g = g0 + pltpu.roll(from_above(g0), LANES - 1, 1) + pltpu.roll(from_below(g0), 1, 1)
    xw = jnp.where((lane >= 120) & (lane < 123), 1.0, g).astype(BF)
    hx = jnp.dot(xw, w1x_ref[0:LANES, :], preferred_element_type=F)
    hx = hx + jnp.dot(xw, w1x_ref[LANES : 2 * LANES, :], preferred_element_type=F)
    live = jnp.where(lane < 32, ends_ref[0], jnp.where(lane >= 96, ends_ref[1], 1))
    hx = jnp.maximum(hx, 0.0) * live.astype(F)
    sums = jnp.dot(hx.astype(BF), w2x_ref[...], preferred_element_type=F)
    hi, lo = settle(lax.rem(lane, 3), sums)
    extra = jnp.dot(hi, sel3_ref[...], preferred_element_type=F) + jnp.dot(lo, sel3_ref[...], preferred_element_type=F)
    copies = []
    for side in range(2):
        held[side] = (part_ref[side] + extra[:, LANES * side : LANES * (side + 1)]).astype(BF)
        block = out_ref.at[:, pl.ds(side * (COLS - LANES), LANES)]
        copies.append(pltpu.make_async_copy(held.at[side], block, sems.at[side]))
        copies[-1].start()
    for copy in copies:
        copy.wait()


SIDE_LANE = {0: 97, 1: 100, COLS - 2: 103, COLS - 1: 106, -2: 109, -1: 112, COLS: 115, COLS + 1: 118}
SIDE_HIDDEN = (-1, 0, COLS - 1, COLS)


def selectors():
    i, l = np.indices((COLS, 2 * LANES))
    i = i % WIN + WIN * (i // (BLOCKS * WIN)) + LANES * (i // WIN % BLOCKS)
    m, s = 16 * (l // LANES) + (l % LANES) // 6, (l % LANES) % 6
    fit = l % LANES < 96
    hit = (fit & (s == 1) & (i == WIN * m - 1)) | (fit & (s == 4) & (i == WIN * m + WIN))
    for c in (0, 1, COLS - 2, COLS - 1):
        hit = hit | ((l == SIDE_LANE[c]) & (i == c))
    sel1 = hit.astype(BF)
    i, l = np.indices((2 * LANES, LANES))
    hit = np.zeros((2 * LANES, LANES), bool)
    for row, c in ((LANES - 2, -2), (LANES - 1, -1), (LANES, COLS), (LANES + 1, COLS + 1)):
        hit = hit | ((i == row) & (l == SIDE_LANE[c]))
    selx = hit.astype(BF)
    l, j = np.indices((2 * LANES, COLS))
    m, s = 16 * (l // LANES) + (l % LANES) // 6, (l % LANES) % 6
    fit = l % LANES < 96
    sel2 = ((fit & (s < 3) & (j == WIN * m - 1)) | (fit & (s >= 3) & (j == WIN * m + WIN))).astype(BF)
    l, j = np.indices((LANES, 2 * LANES))
    hit = np.zeros((LANES, 2 * LANES), bool)
    for n, c in enumerate((0, 1, 2 * LANES - 2, 2 * LANES - 1)):
        hit = hit | ((l // 3 == n) & (j == c))
    return sel1, sel2, selx, hit.astype(BF)


def patterns():
    width = WIN * 32
    rows1, hit1, rowsx, hitx, lanes2, hit2, lanesy, hity = ([] for _ in range(8))
    for b in range(3):
        k, n = np.indices((LANES, width))
        pos, inner = n // 32, k % WIN
        hit1.append(
            ((k < 96) & (inner == pos + b - 1))
            | ((b == 0) & (k >= 96) & (k < 99) & (pos == 0))
            | ((b == 2) & (k >= 99) & (k < 102) & (pos == WIN - 1))
            | ((b == 1) & (k >= 102) & (k < 105))
        )
        k, tap = np.indices((LANES, 16))
        rows1.append(
            ((k < 96) & (tap == 3 * (k // WIN) + b))
            | ((b == 0) & (k >= 96) & (k < 99) & (tap == 3 * (k - 96)))
            | ((b == 2) & (k >= 99) & (k < 102) & (tap == 3 * (k - 99) + 2))
            | ((b == 1) & (k >= 102) & (k < 105) & (tap == k - 102 + 9))
        )
        k, n = np.indices((LANES, LANES))
        hit = (b == 1) & (k >= 120) & (k < 123)
        for h, c in enumerate(SIDE_HIDDEN):
            first = SIDE_LANE[c + b - 1] - 1
            hit = hit | ((n // 32 == h) & (k >= first) & (k < first + 3))
        hitx.append(hit)
        k, tap = np.indices((LANES, 16))
        row = (b == 1) & (k >= 120) & (k < 123) & (tap == k - 120 + 9)
        for middle in SIDE_LANE.values():
            row = row | ((k >= middle - 1) & (k <= middle + 1) & (tap == 3 * (k - middle + 1) + b))
        rowsx.append(row)
        n, l = np.indices((width, LANES))
        pos, inner = n // 32, l % WIN
        hit2.append(
            ((l < 96) & (inner == pos + 1 - b))
            | ((b == 2) & (l >= 96) & (l < 99) & (pos == 0))
            | ((b == 0) & (l >= 99) & (l < 102) & (pos == WIN - 1))
        )
        tap, l = np.indices((16, LANES))
        lanes2.append(
            ((l < 96) & (tap == 3 * (l // WIN) + b))
            | ((b == 2) & (l >= 96) & (l < 99) & (tap == 3 * (l - 96) + 2))
            | ((b == 0) & (l >= 99) & (l < 102) & (tap == 3 * (l - 99)))
        )
        n, l = np.indices((LANES, LANES))
        hit = np.zeros((LANES, LANES), bool)
        for h, c in enumerate(SIDE_HIDDEN):
            for j, out in enumerate((0, 1, COLS - 2, COLS - 1)):
                if c == out + b - 1:
                    hit = hit | ((n // 32 == h) & (l // 3 == j))
        hity.append(hit)
        tap, l = np.indices((16, LANES))
        lanesy.append((l < 12) & (tap == 3 * (l % 3) + b))
    i, n = np.indices((32, width))
    spread = i == n % 32
    groups = (rows1, hit1, rowsx, hitx, lanes2, hit2, lanesy, hity)
    return (spread.astype(BF), spread.T.astype(BF)) + tuple(np.stack(g).astype(BF) for g in groups)


def tables_body(
    first_ref, second_ref, spread_ref, tall_ref, rows1, hit1, rowsx, hitx, lanes2, hit2, lanesy, hity,
    w1_ref, w2_ref, w1x_ref, w2x_ref,
):
    dot = functools.partial(jnp.dot, preferred_element_type=F)
    raw = first_ref[...]
    hi = raw.astype(BF).astype(F)
    mid = (raw - hi).astype(BF).astype(F)
    low = raw - hi - mid
    row = lax.broadcasted_iota(I, raw.shape, 0)
    parts = (
        jnp.where(row == 10, mid, jnp.where(row == 11, low, hi)),
        jnp.where(row < 9, mid, 0.0),
    )
    for n, part in enumerate(parts):
        wide = dot(part.astype(BF), spread_ref[...]).astype(BF)
        at = slice(LANES * n, LANES * (n + 1))
        w1_ref[at, :] = sum(hit1[b].astype(F) * dot(rows1[b], wide) for b in range(3)).astype(BF)
        w1x_ref[at, :] = sum(hitx[b].astype(F) * dot(rowsx[b], wide[:, :LANES]) for b in range(3)).astype(BF)
    second = second_ref[...]
    tall = tall_ref[...]
    base = sum(
        hit2[b].astype(F) * dot(tall, dot(second, lanes2[b]).astype(BF)) for b in range(3)
    )
    for w in range(4):
        turned = pltpu.roll(base, WIN * w, 1) if w else base
        w2_ref[:, LANES * w : LANES * (w + 1)] = turned.astype(BF)
    w2x_ref[...] = sum(
        hity[b].astype(F) * dot(tall[:LANES], dot(second, lanesy[b]).astype(BF)) for b in range(3)
    ).astype(BF)


def weights(w_first, b_first, w_second):
    first = jnp.concatenate([w_first, jnp.broadcast_to(b_first[None], (3, 32)), jnp.zeros((4, 32), F)])
    second = jnp.pad(w_second.T, ((0, 0), (0, 7)))
    consts = patterns()
    vmem = pl.BlockSpec(memory_space=pltpu.VMEM)
    shapes = ((2 * LANES, WIN * 32), (WIN * 32, 4 * LANES), (2 * LANES, LANES), (LANES, LANES))
    return pl.pallas_call(
        tables_body,
        out_shape=tuple(jax.ShapeDtypeStruct(shape, BF) for shape in shapes),
        in_specs=[vmem] * (2 + len(consts)),
        out_specs=(vmem,) * 4,
        compiler_params=pltpu.CompilerParams(vmem_limit_bytes=61 * 1024 * 1024),
        cost_estimate=pl.CostEstimate(flops=0, bytes_accessed=60_000_000, transcendentals=0),
        name="tables",
    )(first, second, *consts)


def refine(mask, scores, tables):
    vmem = pl.BlockSpec(memory_space=pltpu.VMEM)
    return pl.pallas_call(
        refine_body,
        out_shape=(
            jax.ShapeDtypeStruct((ROWS, COLS), BF),
            jax.ShapeDtypeStruct((ROWS, LANES), F),
            jax.ShapeDtypeStruct((2, ROWS, LANES), F),
        ),
        in_specs=[pl.BlockSpec(memory_space=pltpu.SMEM), vmem] + [vmem] * len(tables),
        out_specs=(vmem, vmem, vmem),
        scratch_shapes=[
            pltpu.VMEM((BLOCKS, ROWS, LANES), F),
            pltpu.VMEM((2, ROWS, LANES), F),
            pltpu.VMEM((4 * ROWS * BPI, 2 * LANES), BF),
            pltpu.VMEM((4 * ROWS * BPI, WIN * 32), BF),
            pltpu.VMEM((BLOCKS, ROWS, LANES), F),
            pltpu.VMEM((2, ROWS, LANES), F),
        ],
        compiler_params=pltpu.CompilerParams(vmem_limit_bytes=36 * 1024 * 1024),
        cost_estimate=pl.CostEstimate(flops=9_400_000_000, bytes_accessed=8_000_000, transcendentals=0),
        name="refine",
    )(mask, scores, *tables)


def sides(ends, left, right, own, part, tables, out):
    vmem = pl.BlockSpec(memory_space=pltpu.VMEM)
    any_space = pl.BlockSpec(memory_space=pl.ANY)
    return pl.pallas_call(
        sides_body,
        out_shape=jax.ShapeDtypeStruct((ROWS, COLS), BF),
        in_specs=[pl.BlockSpec(memory_space=pltpu.SMEM)] + [vmem] * 8 + [any_space],
        out_specs=any_space,
        scratch_shapes=[pltpu.VMEM((2, ROWS, LANES), BF), pltpu.SemaphoreType.DMA((2,))],
        input_output_aliases={9: 0},
        compiler_params=pltpu.CompilerParams(vmem_limit_bytes=8 * 1024 * 1024),
        cost_estimate=pl.CostEstimate(flops=60_000_000, bytes_accessed=1_500_000, transcendentals=0),
        name="sides",
    )(ends, left, right, own, part, *tables, out)


def score_body(seat_ref, slab_ref, *rest):
    q_refs, out_ref = rest[:-1], rest[-1]
    side = len(q_refs)
    slab = slab_ref[...].swapaxes(0, 1).reshape(BLOCKS * WIN, slab_ref.shape[3])
    for step, q_ref in enumerate(q_refs):
        v = lax.rem(seat_ref[0] + side - step, side)
        out_ref[v] = lax.dot_general(q_ref[...], slab, NT, preferred_element_type=F).astype(BF)


def score(seat, slab, videos):
    vmem = pl.BlockSpec(memory_space=pltpu.VMEM)
    return pl.pallas_call(
        score_body,
        out_shape=jax.ShapeDtypeStruct((len(videos), ROWS, BLOCKS * WIN), BF),
        in_specs=[pl.BlockSpec(memory_space=pltpu.SMEM), vmem] + [vmem] * len(videos),
        out_specs=vmem,
        compiler_params=pltpu.CompilerParams(vmem_limit_bytes=12 * 1024 * 1024),
        cost_estimate=pl.CostEstimate(flops=540_000_000, bytes_accessed=3_100_000, transcendentals=0),
        name="score",
    )(seat, slab, *videos)


def pack_body(me_ref, time_ref, panels_ref, out_ref, zero_ref, sems):
    me = me_ref[0]
    first = me - lax.rem(me, 2)
    jobs = []
    for i in range(2 * BLOCKS):
        owner = time_ref[first * BLOCKS + i] // BLOCKS
        chip = owner // 2
        chip = jnp.where(lax.rem(me, 2) == 0, chip, out_ref.shape[0] // 2 - 1 - chip)
        slot = 2 * chip + i // BLOCKS
        copy = pltpu.make_async_copy(panels_ref.at[i], out_ref.at[slot], sems.at[i])
        jobs.append((lax.rem(owner, 2) == lax.rem(me, 2), copy))
    for wanted, copy in jobs:
        pl.when(wanted)(copy.start)
    zero_ref[...] = jnp.zeros(zero_ref.shape, F)
    for wanted, copy in jobs:
        pl.when(wanted)(copy.wait)


def pack(me, panel_time, panels, owners):
    any_space = pl.BlockSpec(memory_space=pl.ANY)
    smem = pl.BlockSpec(memory_space=pltpu.SMEM)
    return pl.pallas_call(
        pack_body,
        out_shape=(
            jax.ShapeDtypeStruct((owners,) + panels.shape[1:], BF),
            jax.ShapeDtypeStruct((8, LANES), F),
        ),
        in_specs=[smem, smem, any_space],
        out_specs=(any_space, pl.BlockSpec(memory_space=pltpu.VMEM)),
        scratch_shapes=[pltpu.SemaphoreType.DMA((2 * BLOCKS,))],
        compiler_params=pltpu.CompilerParams(vmem_limit_bytes=4 * 1024 * 1024),
        cost_estimate=pl.CostEstimate(flops=0, bytes_accessed=600_000, transcendentals=0),
        name="pack",
    )(me, panel_time, panels)


def share_body(q_ref, *rest):
    out_ref = rest[-1]
    out_ref[...] = q_ref[...]


def share(queries, after):
    vmem = pl.BlockSpec(memory_space=pltpu.VMEM)
    return pl.pallas_call(
        share_body,
        out_shape=jax.ShapeDtypeStruct(queries.shape, BF),
        in_specs=[vmem] + [pl.BlockSpec(memory_space=pl.ANY)] * len(after),
        out_specs=vmem,
        compiler_params=pltpu.CompilerParams(vmem_limit_bytes=4 * 1024 * 1024),
        cost_estimate=pl.CostEstimate(flops=0, bytes_accessed=1_000_000, transcendentals=0),
        name="share",
    )(queries, *after)


def place_body(source_ref, incoming_ref, *rest):
    out_ref, sems = rest[-2:]
    copies = [
        pltpu.make_async_copy(incoming_ref.at[source_ref[k]], out_ref.at[d, k], sems.at[d, k])
        for k in range(BLOCKS)
        for d in range(out_ref.shape[0])
    ]
    for copy in copies:
        copy.start()
    for copy in copies:
        copy.wait()


def place(source, incoming, copies, ready):
    any_space = pl.BlockSpec(memory_space=pl.ANY)
    piece = incoming.shape[1:]
    return pl.pallas_call(
        place_body,
        out_shape=jax.ShapeDtypeStruct((copies, BLOCKS) + piece, BF),
        in_specs=[pl.BlockSpec(memory_space=pltpu.SMEM)] + [any_space] * (1 + len(ready)),
        out_specs=any_space,
        scratch_shapes=[pltpu.SemaphoreType.DMA((copies, BLOCKS))],
        compiler_params=pltpu.CompilerParams(vmem_limit_bytes=4 * 1024 * 1024),
        cost_estimate=pl.CostEstimate(flops=0, bytes_accessed=400_000_000, transcendentals=0),
        name="place",
    )(source, incoming, *ready)


def shards(queries, ref_panels, cand_mask, panel_time, w_first, b_first, w_second):
    owners = lax.axis_size("ref")
    fan = lax.axis_size("qry")
    me = lax.axis_index("ref")
    up = [(i, i + 1) for i in range(owners - 1)]
    down = [(i + 1, i) for i in range(owners - 1)]
    pairs = [[2 * z, 2 * z + 1] for z in range(owners // 2)]
    lines = [[2 * z + c for z in range(owners // 2)][:: 1 - 2 * c] for c in range(2)]
    side = LANES // WIN
    outer = [[i + side * j for j in range(side)] for i in range(fan // side)]
    inner = [[side * j + i for i in range(side)] for j in range(fan // side)]
    chip = lax.all_gather(ref_panels, "ref", axis=0, tiled=True, axis_index_groups=pairs)
    packed, zero = pack(me[None], panel_time, chip, owners)
    incoming = lax.all_to_all(packed, "ref", 0, 0, tiled=True, axis_index_groups=lines)
    holder = jnp.arange(owners * BLOCKS, dtype=I) // BLOCKS
    mine = panel_time[None, :] == me * BLOCKS + jnp.arange(BLOCKS, dtype=I)[:, None]
    source = jnp.sum(jnp.where(mine, holder[None, :], 0), axis=1)
    source = jnp.where(me % 2 == 0, source, owners - 2 - source + 2 * (source % 2))
    ends = jnp.stack([(me > 0).astype(I), (me < owners - 1).astype(I)])
    w1, w2, w1x, w2x = weights(w_first, b_first, w_second)
    sel1, sel2, selx, sel3 = selectors()

    shared = share(queries, (zero, w2x))
    videos = [shared] + [
        lax.ppermute(
            shared, "qry", [(g[i], g[(i + step) % side]) for g in outer for i in range(side)]
        )
        for step in range(1, side)
    ]
    seat = lax.axis_index("qry") // (fan // side)

    rows = [jnp.repeat(cand_mask[:, c].astype(BF), ROWS // 2)[:, None] for c in (0, BLOCKS - 1)]
    ready = (ends,) + tuple(rows)
    slab = lax.all_to_all(
        place(source, incoming, side, ready), "qry", 0, 0, tiled=True, axis_index_groups=inner
    )
    scores = lax.all_to_all(score(seat[None], slab, videos), "qry", 0, 0, tiled=True, axis_index_groups=outer)
    head = scores[0, :, :LANES] * rows[0]
    tail = scores[side - 1, :, LANES:] * rows[1]
    from_left = lax.ppermute(tail, "ref", up)
    from_right = lax.ppermute(head, "ref", down)
    out, own, part = refine(cand_mask, scores, (sel1, w1, w2, sel2))
    return sides(ends, from_left, from_right, own, part, (w1x, w2x, selx, sel3), out)


def solution(mesh):
    placed = (P("qry", None), P("ref", "qry", None), P("qry", "ref"), P(), P(), P(), P())
    return jax.shard_map(
        shards, mesh=mesh, in_specs=placed, out_specs=P("qry", "ref"), check_vma=False
    )
```

```python
import functools

import jax
import jax.numpy as jnp
import numpy as np
from jax import lax
from jax.experimental import pallas as pl
from jax.experimental.pallas import tpu as pltpu
from jax.sharding import PartitionSpec as P

BF = jnp.bfloat16
F = jnp.float32
I = jnp.int32
NT = (((1,), (1,)), ((), ()))
ROWS = 256
COLS = 1024
BLOCKS = 8
LANES = 128
WIN = 32
BPI = 4


def from_above(v):
    row = lax.broadcasted_iota(I, v.shape, 0)
    return jnp.where(row == 0, 0.0, pltpu.roll(v, 1, 0))


def from_below(v):
    row = lax.broadcasted_iota(I, v.shape, 0)
    n = v.shape[0]
    return jnp.where(row == n - 1, 0.0, pltpu.roll(v, n - 1, 0))


def quarters(lane, four):
    return jnp.where(
        lane < 64,
        jnp.where(lane < 32, four[0], four[1]),
        jnp.where(lane < 96, four[2], four[3]),
    )


def refine_body(
    mask_ref, score_ref, sel1_ref, w1_ref, w2_ref, sel2_ref,
    out_ref, own_ref, part_ref, sims, gg, xs, hs, acc, ee,
):
    lane = lax.broadcasted_iota(I, (ROWS, LANES), 1)
    top = lax.broadcasted_iota(I, (ROWS, LANES), 0) < ROWS // 2
    keep = []
    for half in range(2):
        rows = [quarters(lane, [mask_ref[r, 4 * half + j] for j in range(4)]) for r in range(2)]
        keep.append(jnp.where(top, rows[0], rows[1]).astype(F))
    g0 = jnp.zeros((ROWS, 2 * LANES), F)
    for n in range(BLOCKS):
        half = n % 2
        v = score_ref[n // 2, :, LANES * half : LANES * (half + 1)].astype(F) * keep[half]
        sims[n] = v
        g0 = g0 + jnp.dot(v.astype(BF), sel1_ref[LANES * n : LANES * (n + 1), :], preferred_element_type=F)
    own_ref[...] = g0[:, :LANES]
    g = g0 + pltpu.roll(from_above(g0), 2 * LANES - 1, 1) + pltpu.roll(from_below(g0), 1, 1)
    gg[0] = g[:, :LANES]
    gg[1] = g[:, LANES:]
    group = ROWS * BPI

    zero = jnp.zeros((), BF)

    def step(it, carry):
        ge = gg[it].astype(BF)
        one = jnp.ones((), BF)
        p = []
        for w in range(4):
            s = sims[2 * w + it]
            up = from_above(s).astype(BF)
            dn = from_below(s).astype(BF)
            s = s.astype(BF)
            for b in range(BPI):
                e = pltpu.roll(ge, (96 - 6 * (4 * b + w)) % LANES, 1)
                parts = (
                    pltpu.roll(up, (LANES - WIN * b) % LANES, 1) if b else up,
                    pltpu.roll(s, (LANES + WIN - WIN * b) % LANES, 1) if b != 1 else s,
                    pltpu.roll(dn, (LANES + 2 * WIN - WIN * b) % LANES, 1) if b != 2 else dn,
                    jnp.where(lane < 102, e, one),
                )
                x = quarters(lane, parts)
                at = group * w + ROWS * b
                xs[at : at + ROWS, 0:LANES] = x
                xs[at : at + ROWS, LANES : 2 * LANES] = x
            at = slice(group * w, group * (w + 1))
            x = xs[at, :]
            for n in range(2):
                h = jnp.dot(x, w1_ref[:, 512 * n : 512 * (n + 1)], preferred_element_type=F)
                hs[at, 512 * n : 512 * (n + 1)] = jnp.maximum(h.astype(BF), zero)
            if w == 0:
                hs[0:ROWS, 0:32] = jnp.where(it == 0, zero, hs[0:ROWS, 0:32])
            if w == 3:
                end = slice(4 * group - ROWS, 4 * group), slice(WIN * 32 - 32, WIN * 32)
                hs[end] = jnp.where(it == BLOCKS // BPI - 1, zero, hs[end])
            p.append(jnp.dot(hs[at, :], w2_ref[:, LANES * w : LANES * (w + 1)], preferred_element_type=F))
        tot = jnp.zeros((ROWS, LANES), F)
        for b in range(BPI):
            k = it * BPI + b
            pb = [p[w][ROWS * b : ROWS * (b + 1)] for w in range(4)]
            a0 = quarters(lane, pb)
            a1 = pltpu.roll(quarters(lane, [pb[3], pb[0], pb[1], pb[2]]), LANES - WIN, 1)
            a2 = pltpu.roll(quarters(lane, [pb[2], pb[3], pb[0], pb[1]]), LANES - 2 * WIN, 1)
            acc[k] = a1 + from_above(a0) + from_below(a2)
            for w in range(4):
                at = 6 * (4 * b + w)
                moved = pltpu.roll(pb[w], (at + LANES - WIN * ((w + 3) % 4)) % LANES, 1)
                tot = jnp.where((lane >= at) & (lane < at + 6), moved, tot)
        ee[it] = tot
        return carry

    lax.fori_loop(0, BLOCKS // BPI, step, 0)
    kind = lax.rem(lane, 3)
    his, los = [], []
    for half in range(2):
        hi, lo = settle(kind, ee[half])
        his.append(hi)
        los.append(lo)
    hi = jnp.concatenate(his, axis=1)
    lo = jnp.concatenate(los, axis=1)
    for k in range(0, BLOCKS, 2):
        pick = sel2_ref[:, LANES * k : LANES * (k + 2)]
        extra = jnp.dot(hi, pick, preferred_element_type=F) + jnp.dot(lo, pick, preferred_element_type=F)
        for u in range(2):
            total = acc[k + u] + extra[:, LANES * u : LANES * (u + 1)]
            if k + u == 0:
                part_ref[0] = total
            elif k + u == BLOCKS - 1:
                part_ref[1] = total
            else:
                out_ref[:, LANES * (k + u) : LANES * (k + u + 1)] = total.astype(BF)


def settle(kind, v):
    c = jnp.where(kind == 0, from_above(v), jnp.where(kind == 1, v, from_below(v)))
    hi = c.astype(BF)
    return hi, (c - hi.astype(F)).astype(BF)


def sides_body(
    ends_ref, left_ref, right_ref, own_ref, part_ref, w1x_ref, w2x_ref, selx_ref, sel3_ref, old_ref,
    out_ref, held, sems,
):
    del old_ref
    lane = lax.broadcasted_iota(I, (ROWS, LANES), 1)
    near = jnp.concatenate([left_ref[...], right_ref[...]], axis=1)
    g0 = jnp.where(lane >= 96, own_ref[...], 0.0) + jnp.dot(near, selx_ref[...], preferred_element_type=F)
    g = g0 + pltpu.roll(from_above(g0), LANES - 1, 1) + pltpu.roll(from_below(g0), 1, 1)
    xw = jnp.where((lane >= 120) & (lane < 123), 1.0, g).astype(BF)
    hx = jnp.dot(xw, w1x_ref[0:LANES, :], preferred_element_type=F)
    hx = hx + jnp.dot(xw, w1x_ref[LANES : 2 * LANES, :], preferred_element_type=F)
    live = jnp.where(lane < 32, ends_ref[0], jnp.where(lane >= 96, ends_ref[1], 1))
    hx = jnp.maximum(hx, 0.0) * live.astype(F)
    sums = jnp.dot(hx.astype(BF), w2x_ref[...], preferred_element_type=F)
    hi, lo = settle(lax.rem(lane, 3), sums)
    extra = jnp.dot(hi, sel3_ref[...], preferred_element_type=F) + jnp.dot(lo, sel3_ref[...], preferred_element_type=F)
    copies = []
    for side in range(2):
        held[side] = (part_ref[side] + extra[:, LANES * side : LANES * (side + 1)]).astype(BF)
        block = out_ref.at[:, pl.ds(side * (COLS - LANES), LANES)]
        copies.append(pltpu.make_async_copy(held.at[side], block, sems.at[side]))
        copies[-1].start()
    for copy in copies:
        copy.wait()


SIDE_LANE = {0: 97, 1: 100, COLS - 2: 103, COLS - 1: 106, -2: 109, -1: 112, COLS: 115, COLS + 1: 118}
SIDE_HIDDEN = (-1, 0, COLS - 1, COLS)


def selectors():
    i, l = np.indices((COLS, 2 * LANES))
    i = i % WIN + WIN * (i // (BLOCKS * WIN)) + LANES * (i // WIN % BLOCKS)
    m, s = 16 * (l // LANES) + (l % LANES) // 6, (l % LANES) % 6
    fit = l % LANES < 96
    hit = (fit & (s == 1) & (i == WIN * m - 1)) | (fit & (s == 4) & (i == WIN * m + WIN))
    for c in (0, 1, COLS - 2, COLS - 1):
        hit = hit | ((l == SIDE_LANE[c]) & (i == c))
    sel1 = hit.astype(BF)
    i, l = np.indices((2 * LANES, LANES))
    hit = np.zeros((2 * LANES, LANES), bool)
    for row, c in ((LANES - 2, -2), (LANES - 1, -1), (LANES, COLS), (LANES + 1, COLS + 1)):
        hit = hit | ((i == row) & (l == SIDE_LANE[c]))
    selx = hit.astype(BF)
    l, j = np.indices((2 * LANES, COLS))
    m, s = 16 * (l // LANES) + (l % LANES) // 6, (l % LANES) % 6
    fit = l % LANES < 96
    sel2 = ((fit & (s < 3) & (j == WIN * m - 1)) | (fit & (s >= 3) & (j == WIN * m + WIN))).astype(BF)
    l, j = np.indices((LANES, 2 * LANES))
    hit = np.zeros((LANES, 2 * LANES), bool)
    for n, c in enumerate((0, 1, 2 * LANES - 2, 2 * LANES - 1)):
        hit = hit | ((l // 3 == n) & (j == c))
    return sel1, sel2, selx, hit.astype(BF)


def patterns():
    width = WIN * 32
    rows1, hit1, rowsx, hitx, lanes2, hit2, lanesy, hity = ([] for _ in range(8))
    for b in range(3):
        k, n = np.indices((LANES, width))
        pos, inner = n // 32, k % WIN
        hit1.append(
            ((k < 96) & (inner == pos + b - 1))
            | ((b == 0) & (k >= 96) & (k < 99) & (pos == 0))
            | ((b == 2) & (k >= 99) & (k < 102) & (pos == WIN - 1))
            | ((b == 1) & (k >= 102) & (k < 105))
        )
        k, tap = np.indices((LANES, 16))
        rows1.append(
            ((k < 96) & (tap == 3 * (k // WIN) + b))
            | ((b == 0) & (k >= 96) & (k < 99) & (tap == 3 * (k - 96)))
            | ((b == 2) & (k >= 99) & (k < 102) & (tap == 3 * (k - 99) + 2))
            | ((b == 1) & (k >= 102) & (k < 105) & (tap == k - 102 + 9))
        )
        k, n = np.indices((LANES, LANES))
        hit = (b == 1) & (k >= 120) & (k < 123)
        for h, c in enumerate(SIDE_HIDDEN):
            first = SIDE_LANE[c + b - 1] - 1
            hit = hit | ((n // 32 == h) & (k >= first) & (k < first + 3))
        hitx.append(hit)
        k, tap = np.indices((LANES, 16))
        row = (b == 1) & (k >= 120) & (k < 123) & (tap == k - 120 + 9)
        for middle in SIDE_LANE.values():
            row = row | ((k >= middle - 1) & (k <= middle + 1) & (tap == 3 * (k - middle + 1) + b))
        rowsx.append(row)
        n, l = np.indices((width, LANES))
        pos, inner = n // 32, l % WIN
        hit2.append(
            ((l < 96) & (inner == pos + 1 - b))
            | ((b == 2) & (l >= 96) & (l < 99) & (pos == 0))
            | ((b == 0) & (l >= 99) & (l < 102) & (pos == WIN - 1))
        )
        tap, l = np.indices((16, LANES))
        lanes2.append(
            ((l < 96) & (tap == 3 * (l // WIN) + b))
            | ((b == 2) & (l >= 96) & (l < 99) & (tap == 3 * (l - 96) + 2))
            | ((b == 0) & (l >= 99) & (l < 102) & (tap == 3 * (l - 99)))
        )
        n, l = np.indices((LANES, LANES))
        hit = np.zeros((LANES, LANES), bool)
        for h, c in enumerate(SIDE_HIDDEN):
            for j, out in enumerate((0, 1, COLS - 2, COLS - 1)):
                if c == out + b - 1:
                    hit = hit | ((n // 32 == h) & (l // 3 == j))
        hity.append(hit)
        tap, l = np.indices((16, LANES))
        lanesy.append((l < 12) & (tap == 3 * (l % 3) + b))
    i, n = np.indices((32, width))
    spread = i == n % 32
    groups = (rows1, hit1, rowsx, hitx, lanes2, hit2, lanesy, hity)
    return (spread.astype(BF), spread.T.astype(BF)) + tuple(np.stack(g).astype(BF) for g in groups)


def tables_body(
    first_ref, second_ref, spread_ref, tall_ref, rows1, hit1, rowsx, hitx, lanes2, hit2, lanesy, hity,
    w1_ref, w2_ref, w1x_ref, w2x_ref,
):
    dot = functools.partial(jnp.dot, preferred_element_type=F)
    raw = first_ref[...]
    hi = raw.astype(BF).astype(F)
    mid = (raw - hi).astype(BF).astype(F)
    low = raw - hi - mid
    row = lax.broadcasted_iota(I, raw.shape, 0)
    parts = (
        jnp.where(row == 10, mid, jnp.where(row == 11, low, hi)),
        jnp.where(row < 9, mid, 0.0),
    )
    for n, part in enumerate(parts):
        wide = dot(part.astype(BF), spread_ref[...]).astype(BF)
        at = slice(LANES * n, LANES * (n + 1))
        w1_ref[at, :] = sum(hit1[b].astype(F) * dot(rows1[b], wide) for b in range(3)).astype(BF)
        w1x_ref[at, :] = sum(hitx[b].astype(F) * dot(rowsx[b], wide[:, :LANES]) for b in range(3)).astype(BF)
    second = second_ref[...]
    tall = tall_ref[...]
    base = sum(
        hit2[b].astype(F) * dot(tall, dot(second, lanes2[b]).astype(BF)) for b in range(3)
    )
    for w in range(4):
        turned = pltpu.roll(base, WIN * w, 1) if w else base
        w2_ref[:, LANES * w : LANES * (w + 1)] = turned.astype(BF)
    w2x_ref[...] = sum(
        hity[b].astype(F) * dot(tall[:LANES], dot(second, lanesy[b]).astype(BF)) for b in range(3)
    ).astype(BF)


def weights(w_first, b_first, w_second):
    first = jnp.concatenate([w_first, jnp.broadcast_to(b_first[None], (3, 32)), jnp.zeros((4, 32), F)])
    second = jnp.pad(w_second.T, ((0, 0), (0, 7)))
    consts = patterns()
    vmem = pl.BlockSpec(memory_space=pltpu.VMEM)
    shapes = ((2 * LANES, WIN * 32), (WIN * 32, 4 * LANES), (2 * LANES, LANES), (LANES, LANES))
    return pl.pallas_call(
        tables_body,
        out_shape=tuple(jax.ShapeDtypeStruct(shape, BF) for shape in shapes),
        in_specs=[vmem] * (2 + len(consts)),
        out_specs=(vmem,) * 4,
        compiler_params=pltpu.CompilerParams(vmem_limit_bytes=61 * 1024 * 1024),
        cost_estimate=pl.CostEstimate(flops=0, bytes_accessed=60_000_000, transcendentals=0),
        name="tables",
    )(first, second, *consts)


def refine(mask, scores, tables):
    vmem = pl.BlockSpec(memory_space=pltpu.VMEM)
    return pl.pallas_call(
        refine_body,
        out_shape=(
            jax.ShapeDtypeStruct((ROWS, COLS), BF),
            jax.ShapeDtypeStruct((ROWS, LANES), F),
            jax.ShapeDtypeStruct((2, ROWS, LANES), F),
        ),
        in_specs=[pl.BlockSpec(memory_space=pltpu.SMEM), vmem] + [vmem] * len(tables),
        out_specs=(vmem, vmem, vmem),
        scratch_shapes=[
            pltpu.VMEM((BLOCKS, ROWS, LANES), F),
            pltpu.VMEM((2, ROWS, LANES), F),
            pltpu.VMEM((4 * ROWS * BPI, 2 * LANES), BF),
            pltpu.VMEM((4 * ROWS * BPI, WIN * 32), BF),
            pltpu.VMEM((BLOCKS, ROWS, LANES), F),
            pltpu.VMEM((2, ROWS, LANES), F),
        ],
        compiler_params=pltpu.CompilerParams(vmem_limit_bytes=36 * 1024 * 1024),
        cost_estimate=pl.CostEstimate(flops=9_400_000_000, bytes_accessed=8_000_000, transcendentals=0),
        name="refine",
    )(mask, scores, *tables)


def sides(ends, left, right, own, part, tables, out):
    vmem = pl.BlockSpec(memory_space=pltpu.VMEM)
    any_space = pl.BlockSpec(memory_space=pl.ANY)
    return pl.pallas_call(
        sides_body,
        out_shape=jax.ShapeDtypeStruct((ROWS, COLS), BF),
        in_specs=[pl.BlockSpec(memory_space=pltpu.SMEM)] + [vmem] * 8 + [any_space],
        out_specs=any_space,
        scratch_shapes=[pltpu.VMEM((2, ROWS, LANES), BF), pltpu.SemaphoreType.DMA((2,))],
        input_output_aliases={9: 0},
        compiler_params=pltpu.CompilerParams(vmem_limit_bytes=8 * 1024 * 1024),
        cost_estimate=pl.CostEstimate(flops=60_000_000, bytes_accessed=1_500_000, transcendentals=0),
        name="sides",
    )(ends, left, right, own, part, *tables, out)


def score_body(seat_ref, slab_ref, *rest):
    q_refs, out_ref = rest[:-1], rest[-1]
    side = len(q_refs)
    slab = slab_ref[...].swapaxes(0, 1).reshape(BLOCKS * WIN, slab_ref.shape[3])
    for step, q_ref in enumerate(q_refs):
        v = lax.rem(seat_ref[0] + side - step, side)
        out_ref[v] = lax.dot_general(q_ref[...], slab, NT, preferred_element_type=F).astype(BF)


def score(seat, slab, videos):
    vmem = pl.BlockSpec(memory_space=pltpu.VMEM)
    return pl.pallas_call(
        score_body,
        out_shape=jax.ShapeDtypeStruct((len(videos), ROWS, BLOCKS * WIN), BF),
        in_specs=[pl.BlockSpec(memory_space=pltpu.SMEM), vmem] + [vmem] * len(videos),
        out_specs=vmem,
        compiler_params=pltpu.CompilerParams(vmem_limit_bytes=12 * 1024 * 1024),
        cost_estimate=pl.CostEstimate(flops=540_000_000, bytes_accessed=3_100_000, transcendentals=0),
        name="score",
    )(seat, slab, *videos)


def pack_body(me_ref, time_ref, panels_ref, out_ref, zero_ref, sems):
    me = me_ref[0]
    first = me - lax.rem(me, 2)
    jobs = []
    for i in range(2 * BLOCKS):
        owner = time_ref[first * BLOCKS + i] // BLOCKS
        slot = owner - lax.rem(owner, 2) + i // BLOCKS
        copy = pltpu.make_async_copy(panels_ref.at[i], out_ref.at[slot], sems.at[i])
        jobs.append((lax.rem(owner, 2) == lax.rem(me, 2), copy))
    for wanted, copy in jobs:
        pl.when(wanted)(copy.start)
    zero_ref[...] = jnp.zeros(zero_ref.shape, F)
    for wanted, copy in jobs:
        pl.when(wanted)(copy.wait)


def pack(me, panel_time, panels, owners):
    any_space = pl.BlockSpec(memory_space=pl.ANY)
    smem = pl.BlockSpec(memory_space=pltpu.SMEM)
    return pl.pallas_call(
        pack_body,
        out_shape=(
            jax.ShapeDtypeStruct((owners,) + panels.shape[1:], BF),
            jax.ShapeDtypeStruct((8, LANES), F),
        ),
        in_specs=[smem, smem, any_space],
        out_specs=(any_space, pl.BlockSpec(memory_space=pltpu.VMEM)),
        scratch_shapes=[pltpu.SemaphoreType.DMA((2 * BLOCKS,))],
        compiler_params=pltpu.CompilerParams(vmem_limit_bytes=4 * 1024 * 1024),
        cost_estimate=pl.CostEstimate(flops=0, bytes_accessed=600_000, transcendentals=0),
        name="pack",
    )(me, panel_time, panels)


def share_body(q_ref, *rest):
    out_ref = rest[-1]
    out_ref[...] = q_ref[...]


def share(queries, after):
    vmem = pl.BlockSpec(memory_space=pltpu.VMEM)
    return pl.pallas_call(
        share_body,
        out_shape=jax.ShapeDtypeStruct(queries.shape, BF),
        in_specs=[vmem] + [pl.BlockSpec(memory_space=pl.ANY)] * len(after),
        out_specs=vmem,
        compiler_params=pltpu.CompilerParams(vmem_limit_bytes=4 * 1024 * 1024),
        cost_estimate=pl.CostEstimate(flops=0, bytes_accessed=1_000_000, transcendentals=0),
        name="share",
    )(queries, *after)


def place_body(source_ref, incoming_ref, *rest):
    out_ref, sems = rest[-2:]
    copies = [
        pltpu.make_async_copy(incoming_ref.at[source_ref[k]], out_ref.at[d, k], sems.at[d, k])
        for k in range(BLOCKS)
        for d in range(out_ref.shape[0])
    ]
    for copy in copies:
        copy.start()
    for copy in copies:
        copy.wait()


def place(source, incoming, copies, ready):
    any_space = pl.BlockSpec(memory_space=pl.ANY)
    piece = incoming.shape[1:]
    return pl.pallas_call(
        place_body,
        out_shape=jax.ShapeDtypeStruct((copies, BLOCKS) + piece, BF),
        in_specs=[pl.BlockSpec(memory_space=pltpu.SMEM)] + [any_space] * (1 + len(ready)),
        out_specs=any_space,
        scratch_shapes=[pltpu.SemaphoreType.DMA((copies, BLOCKS))],
        compiler_params=pltpu.CompilerParams(vmem_limit_bytes=4 * 1024 * 1024),
        cost_estimate=pl.CostEstimate(flops=0, bytes_accessed=400_000_000, transcendentals=0),
        name="place",
    )(source, incoming, *ready)


def shards(queries, ref_panels, cand_mask, panel_time, w_first, b_first, w_second):
    owners = lax.axis_size("ref")
    fan = lax.axis_size("qry")
    me = lax.axis_index("ref")
    up = [(i, i + 1) for i in range(owners - 1)]
    down = [(i + 1, i) for i in range(owners - 1)]
    pairs = [[2 * z, 2 * z + 1] for z in range(owners // 2)]
    lines = [[2 * z + c for z in range(owners // 2)] for c in range(2)]
    side = LANES // WIN
    outer = [[i + side * j for j in range(side)] for i in range(fan // side)]
    inner = [[side * j + i for i in range(side)] for j in range(fan // side)]
    chip = lax.all_gather(ref_panels, "ref", axis=0, tiled=True, axis_index_groups=pairs)
    packed, zero = pack(me[None], panel_time, chip, owners)
    incoming = lax.all_to_all(packed, "ref", 0, 0, tiled=True, axis_index_groups=lines)
    holder = jnp.arange(owners * BLOCKS, dtype=I) // BLOCKS
    mine = panel_time[None, :] == me * BLOCKS + jnp.arange(BLOCKS, dtype=I)[:, None]
    source = jnp.sum(jnp.where(mine, holder[None, :], 0), axis=1)
    ends = jnp.stack([(me > 0).astype(I), (me < owners - 1).astype(I)])
    w1, w2, w1x, w2x = weights(w_first, b_first, w_second)
    sel1, sel2, selx, sel3 = selectors()

    shared = share(queries, (zero, w2x))
    videos = [shared] + [
        lax.ppermute(
            shared, "qry", [(g[i], g[(i + step) % side]) for g in outer for i in range(side)]
        )
        for step in range(1, side)
    ]
    seat = lax.axis_index("qry") // (fan // side)

    rows = [jnp.repeat(cand_mask[:, c].astype(BF), ROWS // 2)[:, None] for c in (0, BLOCKS - 1)]
    ready = (ends,) + tuple(rows)
    slab = lax.all_to_all(
        place(source, incoming, side, ready), "qry", 0, 0, tiled=True, axis_index_groups=inner
    )
    scores = lax.all_to_all(score(seat[None], slab, videos), "qry", 0, 0, tiled=True, axis_index_groups=outer)
    head = scores[0, :, :LANES] * rows[0]
    tail = scores[side - 1, :, LANES:] * rows[1]
    from_left = lax.ppermute(tail, "ref", up)
    from_right = lax.ppermute(head, "ref", down)
    out, own, part = refine(cand_mask, scores, (sel1, w1, w2, sel2))
    return sides(ends, from_left, from_right, own, part, (w1x, w2x, selx, sel3), out)


def solution(mesh):
    placed = (P("qry", None), P("ref", "qry", None), P("qry", "ref"), P(), P(), P(), P())
    return jax.shard_map(
        shards, mesh=mesh, in_specs=placed, out_specs=P("qry", "ref"), check_vma=False
    )
```
